256 devices in a mesh: fsdp: 8 (over y, core), tp: 8 (over z), rep: 4 (over x).
Axes of the slice: x: 4, y: 4, z: 8, core: 2. Of those that a mesh axis runs over, the one named last changes fastest.
Arguments:
- train_inputs: bfloat16 [20480, 8192], P(('fsdp', 'rep'), 'tp'), may hold values from -6 to 6
- kv_grads: bfloat16 [20480, 2048], P(('fsdp', 'rep'), 'tp'), may hold values from -0.125 to 0.125
- master: float32 [8192, 2048], P(('fsdp', 'rep'), 'tp'), may hold values from -0.0234375 to 0.0234375
- first_moment: bfloat16 [8192, 2048], P(('fsdp', 'rep'), 'tp'), may hold values from -0.29882812 to 0.29882812
- second_moment: bfloat16 [8192, 2048], P(('fsdp', 'rep'), 'tp'), may hold values from 0.019897461 to 0.31835938
- hidden_states: bfloat16 [4, 1024, 8192], P(None, ('fsdp', 'rep')), may hold values from -18 to 18
- queries: bfloat16 [4, 1024, 8192], P(None, ('fsdp', 'rep'), 'tp'), may hold values from -24 to 24
- kv_cache: bfloat16 [1024, 256, 2048], P(('fsdp', 'rep'), None, 'tp'), may hold values from -24 to 24
- cache_lengths: int32 [1024], P(('fsdp', 'rep')), may hold values from 2 to 256, as said below
Outputs:
- new_master: float32 [8192, 2048], P(('fsdp', 'rep'), 'tp')
- new_first: bfloat16 [8192, 2048], P(('fsdp', 'rep'), 'tp')
- new_second: bfloat16 [8192, 2048], P(('fsdp', 'rep'), 'tp')
- attended: bfloat16 [4, 1024, 8192], P(None, ('fsdp', 'rep'), 'tp')
The draws below stay inside these ranges and needn't reach their ends.
Inputs may be any that keep to these rules, and one draw needn't show every extreme that they name: `cache_lengths`: in the first row of every device's 32 rows all 256 slots are live.
All inputs are finite; a program needn't handle non-finite values.
Results may differ from the reference program's by a relative error of at most 0.0055.
Values may be sent and summed in bfloat16 or wider, within the bound.
No kernel may reach another device: no remote copies, remote signals or barrier semaphores. Data moves between devices by JAX's collectives and lax.ppermute only.
A program may use at most 128 MiB of HBM per device.

```python
import math
import jax
import jax.numpy as jnp
from jax import lax

D = 8192
HEADS = 64
KVH = 8
HD = 128
ROWS_DEV = 32
CTX = 256
STEPS = 4
ADAM_STEP = 100
KVW = 2048
QW = 8192
TOKENS = 20480
ROWS = 1024
N_FSDP = 8
N_REP = 4


def draw_queries(key, part):
    key = jax.random.fold_in(key, 1)
    group = HEADS // KVH
    shape = (STEPS, ROWS, KVH, group, HD)
    values = jnp.clip(jax.random.normal(key, shape, jnp.float32), -6.0, 6.0)
    return values.reshape(STEPS, ROWS, HEADS * HD).astype(jnp.bfloat16)


def draw_kv_cache(key, part):
    key = jax.random.fold_in(key, 2)
    shape = (ROWS, CTX, KVH, 2, HD)
    values = jnp.clip(jax.random.normal(key, shape, jnp.float32), -6.0, 6.0)
    return values.reshape(ROWS, CTX, KVH * 2 * HD).astype(jnp.bfloat16)


def draw_cache_lengths(key, part):
    key = jax.random.fold_in(key, 3)
    longest = min(CTX, max(CTX // 8, 8))
    lengths = jax.random.randint(key, (ROWS,), 2, longest + 1, jnp.int32)
    full_rows = jnp.arange(ROWS, dtype=jnp.int32) % ROWS_DEV == 0
    return jnp.where(full_rows, CTX, lengths).astype(jnp.int32)


def raised(result, stream_key, source, target, shards_of, factor):
    owner, partner = [(jnp.arange(result.shape[axis_at]) // (result.shape[axis_at] // shards_of)).reshape([-1 if axis == axis_at else 1 for axis in range(result.ndim)]) for axis_at in (source, target)]
    chosen = jax.random.permutation(stream_key, shards_of)[partner]
    strong = (owner == chosen) | (owner == (partner + shards_of // 2) % shards_of)
    return jnp.where(strong, factor * result, result)


def steps_of(key, shape, split, low, top_value):
    factor_of, own = 1.0, jax.random.fold_in(key, 6)
    for dim, parts in split:
        heights = jnp.exp(jax.random.uniform(jax.random.fold_in(own, dim), (parts,), jnp.float32, low / len(split), top_value / len(split)))
        factor_of = factor_of * jnp.repeat(heights, shape[dim] // parts).reshape([-1 if axis == dim else 1 for axis in range(len(shape))])
    return factor_of


def bell_draw(own_key, shape, scale, limit, pieces=(), kind=jnp.bfloat16):
    array = scale * jax.random.normal(own_key, shape, jnp.float32)
    if pieces:
        array = array * steps_of(own_key, shape, pieces, -0.22, 0.18)
    return jnp.clip(array, -limit, limit).astype(kind)


def noise_with(stream_key, shape, width, most, split, heavy, held_as=jnp.bfloat16):
    entries = width * jax.random.normal(stream_key, shape, jnp.float32)
    if split:
        entries = entries * steps_of(stream_key, shape, split, -0.22, 0.18)
    return jnp.clip(raised(entries, jax.random.fold_in(stream_key, 3), *heavy), -most, most).astype(held_as)


def setup_inputs(seed: int = 0) -> dict:
    seeds = jax.random.split(jax.random.key(seed), 10)
    train_inputs = noise_with(seeds[0], (TOKENS, D), 1.0, 6.0, ((0, 32), (1, 8)), (0, 1, 32, 2.75))
    kv_grads = bell_draw(seeds[1], (TOKENS, KVW), (3.0 / TOKENS ** 0.5), 0.125, ((0, 32), (1, 8)))
    master = bell_draw(seeds[2], (D, KVW), (9 * D) ** -0.5, 0.0234375, ((0, 32), (1, 8)), jnp.float32)
    first_moment = bell_draw(seeds[3], (D, KVW), 0.05, 0.29882812, ((0, 32), (1, 8)))
    second_moment = jnp.clip(jnp.exp(math.log(0.31835938) - 2.7725887 * jax.random.uniform(seeds[4], (D, KVW), jnp.float32) ** steps_of(seeds[4], (D, KVW), ((0, 32), (1, 8)), -0.2, 0.2)), 0.019897461, 0.31835938).astype(jnp.bfloat16)
    hidden_states = bell_draw(seeds[5], (STEPS, ROWS, D), 3.0, 18.0, ((1, 32),))
    queries = draw_queries(jax.random.fold_in(seeds[9], 71), 0)
    kv_cache = draw_kv_cache(jax.random.fold_in(seeds[9], 71), 0)
    cache_lengths = draw_cache_lengths(jax.random.fold_in(seeds[9], 71), 0)
    return dict(train_inputs=train_inputs, kv_grads=kv_grads, master=master, first_moment=first_moment, second_moment=second_moment, hidden_states=hidden_states, queries=queries, kv_cache=kv_cache, cache_lengths=cache_lengths)


learn_rate = 0.001
beta_one = 0.9
beta_two = 0.95
decay_rate = 0.1
tiny_term = 1e-08

def attend(queries, cache, fresh, lengths):
    steps = queries.shape[0]
    rows = queries.shape[1]
    span = cache.shape[1]
    kv_heads = cache.shape[2] // (2 * HD)
    group = HEADS // KVH
    query_block = queries.astype(jnp.float32).reshape(steps, rows, kv_heads, group, HD)
    cache_block = cache.astype(jnp.float32).reshape(rows, span, kv_heads, 2, HD)
    fresh_block = fresh.astype(jnp.float32).reshape(steps, rows, kv_heads, 2, HD)
    scale = 1.0 / math.sqrt(HD)
    past = jnp.einsum('srkgd,rtkd->srkgt', query_block, cache_block[:, :, :, 0, :]) * scale
    recent = jnp.einsum('srkgd,urkd->srkgu', query_block, fresh_block[:, :, :, 0, :]) * scale
    live = jnp.arange(span, dtype=jnp.int32)[None, :] < lengths.astype(jnp.int32)[:, None]
    causal = jnp.arange(steps, dtype=jnp.int32)[None, :] <= jnp.arange(steps, dtype=jnp.int32)[:, None]
    past = jnp.where(live[None, :, None, None, :], past, -jnp.inf)
    recent = jnp.where(causal[:, None, None, None, :], recent, -jnp.inf)
    top = jnp.maximum(lax.optimization_barrier(jnp.max(past, axis=-1)), lax.optimization_barrier(jnp.max(recent, axis=-1)))
    past_exp = jnp.exp(past - top[..., None])
    recent_exp = jnp.exp(recent - top[..., None])
    total = lax.optimization_barrier(jnp.sum(past_exp, axis=-1)) + lax.optimization_barrier(jnp.sum(recent_exp, axis=-1))
    past_prob = lax.optimization_barrier((past_exp / total[..., None]).astype(jnp.bfloat16)).astype(jnp.float32)
    recent_prob = lax.optimization_barrier((recent_exp / total[..., None]).astype(jnp.bfloat16)).astype(jnp.float32)
    output = jnp.einsum('srkgt,rtkd->srkgd', past_prob, cache_block[:, :, :, 1, :])
    output = output + jnp.einsum('srkgu,urkd->srkgd', recent_prob, fresh_block[:, :, :, 1, :])
    return output.astype(jnp.bfloat16).reshape(steps, rows, kv_heads * group * HD)

def reference(train_inputs, kv_grads, master, first_moment, second_moment, hidden_states, queries, kv_cache, cache_lengths):
    gradient = lax.dot_general(train_inputs, kv_grads, (((0,), (0,)), ((), ())), preferred_element_type=jnp.float32)
    first = beta_one * first_moment.astype(jnp.float32) + (1.0 - beta_one) * gradient
    second = beta_two * second_moment.astype(jnp.float32) + (1.0 - beta_two) * gradient * gradient
    corr_one = 1.0 - beta_one ** ADAM_STEP
    corr_two = 1.0 - beta_two ** ADAM_STEP
    update = first / corr_one / (jnp.sqrt(second / corr_two) + tiny_term) + decay_rate * master
    new_master = master - learn_rate * update
    weight = new_master.astype(jnp.bfloat16)
    flat = hidden_states.reshape(STEPS * ROWS, D)
    new_kv = jnp.dot(flat, weight, preferred_element_type=jnp.float32).astype(jnp.bfloat16)
    new_kv = lax.optimization_barrier(new_kv).reshape(STEPS, ROWS, KVW)
    groups = N_FSDP * N_REP
    query_groups = queries.reshape(STEPS, groups, ROWS_DEV, QW).transpose(1, 0, 2, 3)
    cache_groups = kv_cache.reshape(groups, ROWS_DEV, CTX, KVW)
    fresh_groups = new_kv.reshape(STEPS, groups, ROWS_DEV, KVW).transpose(1, 0, 2, 3)
    length_groups = cache_lengths.reshape(groups, ROWS_DEV)
    outputs = lax.map(lambda items: attend(items[0], items[1], items[2], items[3]), (query_groups, cache_groups, fresh_groups, length_groups))
    attended = outputs.transpose(1, 0, 2, 3).reshape(STEPS, ROWS, QW)
    return (new_master, first.astype(jnp.bfloat16), second.astype(jnp.bfloat16), attended)
```

```python
import functools
import math

import jax
import jax.numpy as jnp
from jax import lax
from jax.experimental import pallas as pl
from jax.experimental.pallas import tpu as pltpu
from jax.sharding import PartitionSpec as P

HEADS = 64
KVH = 8
HD = 128
ADAM_STEP = 100

learn_rate = 0.001
beta_one = 0.9
beta_two = 0.95
decay_rate = 0.1
tiny_term = 1e-08

NY, NX, NZ = 4, 4, 8
AXES = ("fsdp", "tp", "rep")
VMEM_LIMIT = 40 * 1024 * 1024
f32 = jnp.float32
bf16 = jnp.bfloat16


def pairs_of(move):
    pairs = []
    for y in range(NY):
        for k in range(2):
            for x in range(NX):
                for z in range(NZ):
                    v, j, u, w = move(y, k, x, z)
                    source = ((y * 2 + k) * NZ + z) * NX + x
                    target = (((v % NY) * 2 + j) * NZ + w % NZ) * NX + u % NX
                    pairs.append((source, target))
    return pairs


def swap_core(a):
    return lax.ppermute(a, AXES, pairs_of(lambda y, k, x, z: (y, 1 - k, x, z)))


def shift_z(a, d):
    return lax.ppermute(a, AXES, pairs_of(lambda y, k, x, z: (y, k, x, z + d)))


def shift_first(a, d):
    return lax.ppermute(
        a, AXES, pairs_of(lambda y, k, x, z: (y, k, x + d, z) if k == 0 else (y + d, k, x, z))
    )


def shift_second(a, d):
    return lax.ppermute(
        a, AXES, pairs_of(lambda y, k, x, z: (y + d, k, x, z) if k == 0 else (y, k, x + d, z))
    )


def shift_fsdp(a, d):
    def move(y, k, x, z):
        f = (y * 2 + k + d) % 8
        return f // 2, f % 2, x, z

    return lax.ppermute(a, AXES, pairs_of(move))


def call(kernel, out, args, scratch=(), place=None):
    specs = []
    for a in args:
        if a is place:
            specs.append(pl.BlockSpec(memory_space=pltpu.SMEM))
        else:
            specs.append(pl.BlockSpec(memory_space=pltpu.VMEM))
    return pl.pallas_call(
        kernel,
        out_shape=out,
        in_specs=specs,
        out_specs=jax.tree.map(lambda _: pl.BlockSpec(memory_space=pltpu.VMEM), out),
        scratch_shapes=list(scratch),
        compiler_params=pltpu.CompilerParams(vmem_limit_bytes=VMEM_LIMIT),
    )(*args)


def shape(dims, dtype):
    return jax.ShapeDtypeStruct(dims, dtype)


def partial_kernel(n, place, *refs):
    own_x, other_x = refs[0], refs[1]
    blocks = refs[2 : 2 + 2 * n]
    keep = refs[2 + 2 * n]
    sends = refs[3 + 2 * n : 6 + 2 * n]
    tiles = refs[6 + 2 * n]
    k, p = place[0], place[1]
    over = (((0,), (0,)), ((), ()))
    for i in range(n):
        for a in range(4):
            at = slice(a * 256, a * 256 + 256)
            tile = lax.dot_general(
                blocks[2 * i][...], own_x[:, at], over, preferred_element_type=f32
            ) + lax.dot_general(
                blocks[2 * i + 1][...], other_x[:, at], over, preferred_element_type=f32
            )
            tiles[a] = tile.reshape(4, 32, 256)
        for d in range(4):
            m = lax.rem(p + d, 4)
            for j in range(4):
                a = jnp.where(k == 0, m, j)
                b = jnp.where(k == 0, j, m)
                part = tiles[a, b]
                if d == 0:
                    keep[i, j] = part
                else:
                    sends[d - 1][i, j] = part.astype(bf16)


def middle_kernel(n, place, keep, one, two, three, own, s_one, s_two, s_three, total):
    q = place[2]
    total[...] = (
        keep[...] + one[...].astype(f32) + two[...].astype(f32) + three[...].astype(f32)
    )
    for i in range(n):
        for d, out in enumerate((own, s_one, s_two, s_three)):
            out[i] = total[i, lax.rem(q + d, 4)]


def deal_kernel(place, *refs):
    pieces, outs, held = refs[:8], refs[8:16], refs[16]
    f, z = place[3], place[4]
    for m in range(8):
        held[m] = pieces[m][...]
    for j in range(8):
        outs[j][...] = held[lax.rem(f + j + 8 - z, 8)]


def adam_kernel(place, *refs):
    pieces = refs[:8]
    master, first_moment, second_moment = refs[8:11]
    new_master, new_first, new_second, weight = refs[11:15]
    held = refs[15]
    f = place[3]
    for j in range(8):
        g = lax.rem(f + 8 - j, 8)
        held[lax.rem(g, 2) * 4 + lax.div(g, 2)] = pieces[j][...]
    gradient = held[...].reshape(256, 256).T
    first = beta_one * first_moment[...].astype(f32) + (1.0 - beta_one) * gradient
    second = beta_two * second_moment[...].astype(f32) + (1.0 - beta_two) * gradient * gradient
    corr_one = 1.0 - beta_one**ADAM_STEP
    corr_two = 1.0 - beta_two**ADAM_STEP
    update = first / corr_one / (jnp.sqrt(second / corr_two) + tiny_term)
    update = update + decay_rate * master[...]
    result = master[...] - learn_rate * update
    new_master[...] = result
    new_first[...] = first.astype(bf16)
    new_second[...] = second.astype(bf16)
    weight[...] = result.astype(bf16)


def project_kernel(n, states, *refs):
    weights, out = refs[:n], refs[n]
    total = None
    for i in range(n):
        w = weights[i][...]
        term = jnp.dot(states[i], w, preferred_element_type=f32)
        total = term if total is None else total + term
    out[...] = total


def finish_kernel(mine, theirs, queries, peak, mass, past, out):
    fresh = (mine[...] + theirs[...]).astype(bf16)
    n = fresh.shape[0]
    rows = n // 4
    line = lax.broadcasted_iota(jnp.int32, (n, n), 0)
    lane = lax.broadcasted_iota(jnp.int32, (n, n), 1)
    seen = (lax.rem(line, rows) == lax.rem(lane, rows)) & (lane <= line)
    scale = 1.0 / math.sqrt(HD)
    keys, values = fresh[:, :HD], fresh[:, HD:]
    for g in range(HEADS // KVH):
        at = slice(g * HD, g * HD + HD)
        scores = lax.dot_general(
            queries[:, at], keys, (((1,), (1,)), ((), ())), preferred_element_type=f32
        )
        scores = jnp.where(seen, scores * scale, -1e30)
        before = peak[:, g : g + 1]
        top = jnp.maximum(before, jnp.max(scores, axis=1, keepdims=True))
        weight = jnp.where(seen, jnp.exp(scores - top), 0.0)
        fade = jnp.exp(before - top)
        total = mass[:, g : g + 1] * fade + jnp.sum(weight, axis=1, keepdims=True)
        probs = (weight / total).astype(bf16)
        result = jnp.dot(probs, values, preferred_element_type=f32)
        out[:, at] = (result + past[:, at] * (fade / total)).astype(bf16)


def past_part(queries, cache, lengths):
    steps, rows = queries.shape[0], queries.shape[1]
    span = cache.shape[1]
    group = HEADS // KVH
    block = queries.reshape(steps, rows, group, HD)
    scores = jnp.einsum(
        "srgd,rtd->srgt", block, cache[:, :, :HD], preferred_element_type=f32
    ) * (1.0 / math.sqrt(HD))
    live = jnp.arange(span, dtype=jnp.int32)[None, :] < lengths[:, None]
    scores = jnp.where(live[None, :, None, :], scores, -jnp.inf)
    peak = jnp.max(scores, axis=-1)
    weight = jnp.exp(scores - peak[..., None])
    mass = jnp.sum(weight, axis=-1)
    past = jnp.einsum(
        "srgt,rtd->srgd", weight.astype(bf16), cache[:, :, HD:], preferred_element_type=f32
    )
    n = steps * rows
    return peak.reshape(n, group), mass.reshape(n, group), past.reshape(n, group * HD)


def body(
    train_inputs,
    kv_grads,
    master,
    first_moment,
    second_moment,
    hidden_states,
    queries,
    kv_cache,
    cache_lengths,
):
    f = lax.axis_index("fsdp")
    x = lax.axis_index("rep")
    z = lax.axis_index("tp")
    y, k = f // 2, f % 2
    p = jnp.where(k == 0, x, y)
    q = jnp.where(k == 0, y, x)
    place = jnp.stack([k, p, q, f, z]).astype(jnp.int32)
    tokens = train_inputs.shape[0]

    mine = lax.dynamic_slice(kv_grads, (0, k * 128), (tokens, 128))
    given = lax.dynamic_slice(kv_grads, (0, (1 - k) * 128), (tokens, 128))
    theirs = swap_core(given)
    other_x = swap_core(train_inputs)

    steps, rows, width = hidden_states.shape
    count = steps * rows
    flat = hidden_states.reshape(count, 4, 2, width // 8)
    kept = lax.dynamic_index_in_dim(flat, k, 2, keepdims=False)
    sent = lax.dynamic_index_in_dim(flat, 1 - k, 2, keepdims=False)
    came = swap_core(sent)
    both = jnp.concatenate([kept, came], axis=0).reshape(2 * count, 4, 4, 256)
    grid = both.transpose(1, 2, 0, 3)
    grid = jnp.where(k == 0, grid.transpose(1, 0, 2, 3), grid)
    grid = jnp.concatenate([grid, grid], axis=0)
    grid = lax.dynamic_slice_in_dim(grid, p, 4, axis=0)
    grid = jnp.concatenate([grid, grid], axis=1)
    grid = lax.dynamic_slice_in_dim(grid, q, 4, axis=1)

    peak, mass, past = past_part(queries, kv_cache, cache_lengths)

    def reduce_blocks(blocks):
        n = len(blocks) // 2
        part = (n, 4, 32, 256)
        keep, one, two, three = call(
            functools.partial(partial_kernel, n),
            (shape(part, f32), shape(part, bf16), shape(part, bf16), shape(part, bf16)),
            (place, train_inputs, other_x, *blocks),
            [pltpu.VMEM((4, 4, 32, 256), f32)],
            place,
        )
        one, two, three = shift_first(one, 1), shift_first(two, 2), shift_first(three, 3)
        piece = shape((n, 32, 256), f32)
        own, one, two, three = call(
            functools.partial(middle_kernel, n),
            (piece, piece, piece, piece),
            (place, keep, one, two, three),
            [pltpu.VMEM(part, f32)],
            place,
        )
        one, two, three = shift_second(one, 1), shift_second(two, 2), shift_second(three, 3)
        total = own + one + two + three
        return [total[i] for i in range(n)]

    pieces = [None] * 8
    pieces[0] = reduce_blocks((mine, theirs))[0]
    right = (mine, theirs)
    left = (mine, theirs)
    for s in (1, 2, 3):
        right = tuple(shift_z(a, 1) for a in right)
        left = tuple(shift_z(a, -1) for a in left)
        back, forth = reduce_blocks((*right, *left))
        pieces[s] = shift_z(back, -s)
        pieces[8 - s] = shift_z(forth, s)
    far = (shift_z(right[0], 1), shift_z(left[1], -1))
    pieces[4] = shift_z(reduce_blocks(far)[0], 4)

    piece = shape((32, 256), f32)
    dealt = call(
        deal_kernel,
        (piece,) * 8,
        (place, *pieces),
        [pltpu.VMEM((8, 32, 256), f32)],
        place,
    )
    dealt = [dealt[0]] + [shift_fsdp(dealt[j], j) for j in range(1, 8)]
    square = (256, 256)
    new_master, new_first, new_second, weight = call(
        adam_kernel,
        (shape(square, f32), shape(square, bf16), shape(square, bf16), shape(square, bf16)),
        (place, *dealt, master, first_moment, second_moment),
        [pltpu.VMEM((8, 32, 256), f32)],
        place,
    )

    def ring(own, shift):
        behind = shift(own, 1)
        ahead = shift(own, -1)
        half = own.shape[0] // 2
        far_top = shift(behind[:half], 1)
        far_low = shift(ahead[half:], -1)
        return own, ahead, jnp.concatenate([far_top, far_low], axis=0), behind

    blocks = []
    for w in ring(weight, shift_first):
        blocks.extend(ring(w, shift_second))
    product = call(
        functools.partial(project_kernel, 16),
        shape((2 * count, 256), f32),
        (grid.reshape(16, 2 * count, 256), *blocks),
    )
    got = swap_core(product[count:])
    attended = call(
        finish_kernel,
        shape((count, queries.shape[2]), bf16),
        (product[:count], got, queries.reshape(count, queries.shape[2]), peak, mass, past),
    )
    return new_master, new_first, new_second, attended.reshape(queries.shape)


def solution(mesh):
    in_specs = (
        P(("fsdp", "rep"), "tp"),
        P(("fsdp", "rep"), "tp"),
        P(("fsdp", "rep"), "tp"),
        P(("fsdp", "rep"), "tp"),
        P(("fsdp", "rep"), "tp"),
        P(None, ("fsdp", "rep"), None),
        P(None, ("fsdp", "rep"), "tp"),
        P(("fsdp", "rep"), None, "tp"),
        P(("fsdp", "rep")),
    )
    out_specs = (
        P(("fsdp", "rep"), "tp"),
        P(("fsdp", "rep"), "tp"),
        P(("fsdp", "rep"), "tp"),
        P(None, ("fsdp", "rep"), "tp"),
    )
    return jax.shard_map(body, mesh=mesh, in_specs=in_specs, out_specs=out_specs, check_vma=False)
```

```python
import functools
import math

import jax
import jax.numpy as jnp
from jax import lax
from jax.experimental import pallas as pl
from jax.experimental.pallas import tpu as pltpu
from jax.sharding import PartitionSpec as P

HEADS = 64
KVH = 8
HD = 128
ADAM_STEP = 100

learn_rate = 0.001
beta_one = 0.9
beta_two = 0.95
decay_rate = 0.1
tiny_term = 1e-08

NY, NX, NZ = 4, 4, 8
AXES = ("fsdp", "tp", "rep")
VMEM_LIMIT = 40 * 1024 * 1024
f32 = jnp.float32
bf16 = jnp.bfloat16


def pairs_of(move):
    pairs = []
    for y in range(NY):
        for k in range(2):
            for x in range(NX):
                for z in range(NZ):
                    v, j, u, w = move(y, k, x, z)
                    source = ((y * 2 + k) * NZ + z) * NX + x
                    target = (((v % NY) * 2 + j) * NZ + w % NZ) * NX + u % NX
                    pairs.append((source, target))
    return pairs


def swap_core(a):
    return lax.ppermute(a, AXES, pairs_of(lambda y, k, x, z: (y, 1 - k, x, z)))


def pass_on(a):
    return lax.ppermute(a, AXES, pairs_of(lambda y, k, x, z: (y, k, x, z + 1 - 2 * k)))


def shift_first(a, d):
    return lax.ppermute(
        a, AXES, pairs_of(lambda y, k, x, z: (y, k, x + d, z) if k == 0 else (y + d, k, x, z))
    )


def shift_second(a, d):
    return lax.ppermute(
        a, AXES, pairs_of(lambda y, k, x, z: (y + d, k, x, z) if k == 0 else (y, k, x + d, z))
    )


def to_column(a):
    return lax.ppermute(a, AXES, pairs_of(lambda y, k, x, z: (y, k, x, z + 4 * k - y)))


def to_owner(a):
    def move(y, k, x, z):
        t = (z + y + 4 * k) % 8
        return t // 2, t % 2, x, z

    return lax.ppermute(a, AXES, pairs_of(move))


SMEM = pl.BlockSpec(memory_space=pltpu.SMEM)
VMEM = pl.BlockSpec(memory_space=pltpu.VMEM)
ANY = pl.BlockSpec(memory_space=pl.ANY)


def call(kernel, out, args, in_specs, out_specs, scratch=(), aliases=None, flops=0, moved=0):
    return pl.pallas_call(
        kernel,
        out_shape=out,
        in_specs=in_specs,
        out_specs=out_specs,
        scratch_shapes=list(scratch),
        input_output_aliases=aliases or {},
        cost_estimate=pl.CostEstimate(flops=flops, bytes_accessed=moved, transcendentals=0),
        compiler_params=pltpu.CompilerParams(vmem_limit_bytes=VMEM_LIMIT),
    )(*args)


def shape(dims, dtype):
    return jax.ShapeDtypeStruct(dims, dtype)


def after_all(value, *others):
    def kernel(*refs):
        pass

    return call(
        kernel,
        shape(value.shape, value.dtype),
        (value, *others),
        [ANY] * (1 + len(others)),
        ANY,
        aliases={0: 0},
    )


def partial_kernel(step, first, *refs):
    place, own_x, other_x, block, other_block = refs[:5]
    refs = refs[5:] if first else refs[9:]
    keep, one, two, three, token, wide, narrow, sems = refs
    k, p = place[0], place[1]
    slot = jnp.where(k == 0, step, 4 - step)
    over = (((0,), (0,)), ((), ()))
    token[...] = jnp.zeros_like(token)

    @pl.when((slot >= 0) & (slot < 4))
    def _():
        for a in range(4):
            at = slice(a * 256, a * 256 + 256)
            tile = lax.dot_general(
                block[...], own_x[:, at], over, preferred_element_type=f32
            ) + lax.dot_general(
                other_block[...], other_x[:, at], over, preferred_element_type=f32
            )
            wide[a] = tile
            narrow[a] = tile.astype(bf16)
            d = lax.rem(jnp.where(k == 0, a, slot) - p + 4, 4)
            index = jnp.where(k == 0, slot, a)

            @pl.when(d == 0)
            def _():
                pltpu.make_async_copy(wide.at[a], keep.at[index], sems.at[a]).start()

            for m, out in ((1, one), (2, two), (3, three)):

                @pl.when(d == m)
                def _():
                    pltpu.make_async_copy(narrow.at[a], out.at[index], sems.at[a]).start()

        for a in range(4):
            d = lax.rem(jnp.where(k == 0, a, slot) - p + 4, 4)
            index = jnp.where(k == 0, slot, a)

            @pl.when(d == 0)
            def _():
                pltpu.make_async_copy(wide.at[a], keep.at[index], sems.at[a]).wait()

            for m, out in ((1, one), (2, two), (3, three)):

                @pl.when(d == m)
                def _():
                    pltpu.make_async_copy(narrow.at[a], out.at[index], sems.at[a]).wait()


def middle_kernel(place, keep, one, two, three, *refs):
    own, s_one, s_two, s_three = refs[3:]
    q = place[2]
    for d, out in enumerate((own, s_one, s_two, s_three)):
        j = lax.rem(q + d, 4)
        out[...] = (
            keep[j] + one[j].astype(f32) + two[j].astype(f32) + three[j].astype(f32)
        )


def adam_kernel(gradient, master, first_moment, second_moment, *outs):
    new_master, new_first, new_second, weight = outs
    gradient = gradient[...].astype(f32).T
    first = beta_one * first_moment[...].astype(f32) + (1.0 - beta_one) * gradient
    second = beta_two * second_moment[...].astype(f32) + (1.0 - beta_two) * gradient * gradient
    corr_one = 1.0 - beta_one**ADAM_STEP
    corr_two = 1.0 - beta_two**ADAM_STEP
    update = first / corr_one / (jnp.sqrt(second / corr_two) + tiny_term)
    update = update + decay_rate * master[...]
    result = master[...] - learn_rate * update
    new_master[...] = result
    new_first[...] = first.astype(bf16)
    new_second[...] = second.astype(bf16)
    weight[...] = result.astype(bf16)


def states_kernel(place, states, kept, sent):
    k, p, q = place[0], place[1], place[2]
    for m in range(4):
        for n in range(4):
            for core, a, b, out in ((k, p, q, kept), (1 - k, q, p, sent)):
                u, v = lax.rem(a + m, 4), lax.rem(b + n, 4)
                x = jnp.where(core == 0, u, v)
                y = jnp.where(core == 0, v, u)
                at = pl.multiple_of(((2 * y + core) * 4 + x) * 256, 256)
                out[m + 4 * n] = states[:, pl.ds(at, 256)]


def project_kernel(base, n, has, kept, came, *refs):
    weights = refs[:n]
    if has:
        before_mine, before_theirs = refs[n : n + 2]
    mine, theirs = refs[-2:]
    total, other = None, None
    if has:
        total, other = before_mine[...], before_theirs[...]
    for i in range(n):
        for m in range(4):
            w = weights[i][m]
            at = base[i] * 4 + m
            term = jnp.dot(kept[at], w, preferred_element_type=f32)
            total = term if total is None else total + term
            term = jnp.dot(came[at], w, preferred_element_type=f32)
            other = term if other is None else other + term
    mine[...] = total
    theirs[...] = other


def finish_kernel(mine, theirs, queries, peak, mass, past, out):
    fresh = (mine[...] + theirs[...]).astype(bf16)
    n = fresh.shape[0]
    rows = n // 4
    group = HEADS // KVH
    line = lax.broadcasted_iota(jnp.int32, (n, n), 0)
    lane = lax.broadcasted_iota(jnp.int32, (n, n), 1)
    seen = (lax.rem(line, rows) == lax.rem(lane, rows)) & (lane <= line)
    seen = jnp.concatenate([seen.astype(f32)] * group, axis=0) > 0.5
    scale = 1.0 / math.sqrt(HD)
    keys, values = fresh[:, :HD], fresh[:, HD:]
    stack = jnp.concatenate([queries[:, g * HD : g * HD + HD] for g in range(group)], axis=0)
    scores = lax.dot_general(
        stack, keys, (((1,), (1,)), ((), ())), preferred_element_type=f32
    )
    scores = jnp.where(seen, scores * scale, -1e30)
    before = jnp.concatenate([peak[:, g : g + 1] for g in range(group)], axis=0)
    mass = jnp.concatenate([mass[:, g : g + 1] for g in range(group)], axis=0)
    top = jnp.maximum(before, jnp.max(scores, axis=1, keepdims=True))
    weight = jnp.where(seen, jnp.exp(scores - top), 0.0)
    fade = jnp.exp(before - top)
    total = mass * fade + jnp.sum(weight, axis=1, keepdims=True)
    probs = (weight / total).astype(bf16)
    result = jnp.dot(probs, values, preferred_element_type=f32)
    result = (result + past[...] * (fade / total)).astype(bf16)
    for g in range(group):
        out[:, g * HD : g * HD + HD] = result[g * n : g * n + n]


def past_part(queries, cache, lengths):
    steps, rows = queries.shape[0], queries.shape[1]
    span = cache.shape[1]
    group = HEADS // KVH
    block = queries.reshape(steps, rows, group, HD)
    scores = jnp.einsum(
        "srgd,rtd->srgt", block, cache[:, :, :HD], preferred_element_type=f32
    ) * (1.0 / math.sqrt(HD))
    live = jnp.arange(span, dtype=jnp.int32)[None, :] < lengths[:, None]
    scores = jnp.where(live[None, :, None, :], scores, -jnp.inf)
    peak = jnp.max(scores, axis=-1)
    weight = jnp.exp(scores - peak[..., None])
    mass = jnp.sum(weight, axis=-1)
    past = jnp.einsum(
        "srgt,rtd->gsrd", weight.astype(bf16), cache[:, :, HD:], preferred_element_type=f32
    )
    n = steps * rows
    return peak.reshape(n, group), mass.reshape(n, group), past.reshape(n * group, HD)


def body(
    train_inputs,
    kv_grads,
    master,
    first_moment,
    second_moment,
    hidden_states,
    queries,
    kv_cache,
    cache_lengths,
):
    f = lax.axis_index("fsdp")
    x = lax.axis_index("rep")
    y, k = f // 2, f % 2
    p = jnp.where(k == 0, x, y)
    q = jnp.where(k == 0, y, x)
    place = jnp.stack([k, p, q]).astype(jnp.int32)
    steps, rows, width = hidden_states.shape
    count = steps * rows

    block = kv_grads
    other_block = swap_core(kv_grads)
    other_x = swap_core(train_inputs)

    part = (4, 256, 256)
    buffers = ()
    outs = (shape(part, f32),) + (shape(part, bf16),) * 3 + (shape((8, 128), f32),)

    def add_slot(step, block, other_block, buffers):
        first = not buffers
        *buffers, token = call(
            functools.partial(partial_kernel, step, first),
            outs,
            (place, train_inputs, other_x, block, other_block, *buffers),
            [SMEM] + [VMEM] * 4 + [ANY] * len(buffers),
            [ANY] * 4 + [VMEM],
            [
                pltpu.VMEM(part, f32),
                pltpu.VMEM(part, bf16),
                pltpu.SemaphoreType.DMA((4,)),
            ],
            {} if first else {5: 0, 6: 1, 7: 2, 8: 3},
            flops=4 * 640 * 1024 * 256,
            moved=6 << 20,
        )
        return tuple(buffers), token

    kept, sent = call(
        states_kernel,
        (shape((16, count, 256), bf16),) * 2,
        (place, hidden_states.reshape(count, width)),
        [SMEM, VMEM],
        [VMEM, VMEM],
        moved=4 << 20,
    )
    tokens = []
    arrived = (block, other_block)
    for step in range(5):
        if step == 1:
            arrived = (after_all(arrived[0], kept), arrived[1])
        if step == 2:
            arrived = (after_all(arrived[0], tokens[0]), arrived[1])
        if step == 3:
            arrived = (after_all(arrived[0], tokens[1]), arrived[1])
        if step < 4:
            after = (pass_on(arrived[0]), pass_on(arrived[1]))
        buffers, token = add_slot(step, *arrived, buffers)
        tokens.append(token)
        arrived = after
    came = swap_core(sent)

    keep, one, two, three = buffers
    peak, mass, past = past_part(queries, kv_cache, cache_lengths)
    one, two, three = shift_first(one, 1), shift_first(two, 2), shift_first(three, 3)
    square = shape((256, 256), f32)
    own, one, two, three = call(
        middle_kernel,
        (square,) * 4,
        (place, keep, one, two, three, past, peak, mass),
        [SMEM] + [VMEM] * 4 + [ANY] * 3,
        [VMEM] * 4,
        moved=4 << 20,
    )
    one, two, three = shift_second(one, 1), shift_second(two, 2), shift_second(three, 3)
    gradient = (own + one + two + three).astype(bf16)
    gradient = to_owner(to_column(gradient))
    narrow = shape((256, 256), bf16)
    new_master, new_first, new_second, weight = call(
        adam_kernel,
        (square, narrow, narrow, narrow),
        (gradient, master, first_moment, second_moment),
        [VMEM] * 4,
        [VMEM] * 4,
        moved=1 << 20,
    )

    stack = jnp.stack(
        [weight, shift_first(weight, -1), shift_first(weight, 2), shift_first(weight, 1)]
    )
    ahead, across, behind = shift_second(stack, -1), shift_second(stack, 2), shift_second(stack, 1)
    result = (shape((count, 256), f32),) * 2

    def project(base, weights, before):
        return call(
            functools.partial(project_kernel, base, len(base), bool(before)),
            result,
            (kept, came, *weights, *before),
            [VMEM] * (2 + len(base) + len(before)),
            [VMEM] * 2,
            flops=len(base) * 4 * 4 * 128 * 256 * 256,
            moved=len(base) << 19,
        )

    sums = project((0,), (stack,), ())
    sums = project((1, 3), (ahead, behind), sums)
    mine, theirs = project((2,), (across,), sums)
    got = swap_core(theirs)
    attended = call(
        finish_kernel,
        shape((count, queries.shape[2]), bf16),
        (mine, got, queries.reshape(count, queries.shape[2]), peak, mass, past),
        [VMEM] * 6,
        VMEM,
        moved=1 << 20,
    )
    return new_master, new_first, new_second, attended.reshape(queries.shape)


def solution(mesh):
    in_specs = (
        P(("fsdp", "rep"), "tp"),
        P(("fsdp", "rep"), "tp"),
        P(("fsdp", "rep"), "tp"),
        P(("fsdp", "rep"), "tp"),
        P(("fsdp", "rep"), "tp"),
        P(None, ("fsdp", "rep"), None),
        P(None, ("fsdp", "rep"), "tp"),
        P(("fsdp", "rep"), None, "tp"),
        P(("fsdp", "rep")),
    )
    out_specs = (
        P(("fsdp", "rep"), "tp"),
        P(("fsdp", "rep"), "tp"),
        P(("fsdp", "rep"), "tp"),
        P(None, ("fsdp", "rep"), "tp"),
    )
    return jax.shard_map(body, mesh=mesh, in_specs=in_specs, out_specs=out_specs, check_vma=False)
```

```python
import functools
import math

import jax
import jax.numpy as jnp
from jax import lax
from jax.experimental import pallas as pl
from jax.experimental.pallas import tpu as pltpu
from jax.sharding import PartitionSpec as P

HEADS = 64
KVH = 8
HD = 128
ADAM_STEP = 100

learn_rate = 0.001
beta_one = 0.9
beta_two = 0.95
decay_rate = 0.1
tiny_term = 1e-08

NY, NX, NZ = 4, 4, 8
AXES = ("fsdp", "tp", "rep")
VMEM_LIMIT = 40 * 1024 * 1024
f32 = jnp.float32
bf16 = jnp.bfloat16


def pairs_of(move):
    pairs = []
    for y in range(NY):
        for k in range(2):
            for x in range(NX):
                for z in range(NZ):
                    v, j, u, w = move(y, k, x, z)
                    source = ((y * 2 + k) * NZ + z) * NX + x
                    target = (((v % NY) * 2 + j) * NZ + w % NZ) * NX + u % NX
                    pairs.append((source, target))
    return pairs


def swap_core(a):
    return lax.ppermute(a, AXES, pairs_of(lambda y, k, x, z: (y, 1 - k, x, z)))


def pass_on(a):
    return lax.ppermute(a, AXES, pairs_of(lambda y, k, x, z: (y, k, x, z + 1 - 2 * k)))


def shift_first(a, d):
    return lax.ppermute(
        a, AXES, pairs_of(lambda y, k, x, z: (y, k, x + d, z) if k == 0 else (y + d, k, x, z))
    )


def shift_second(a, d):
    return lax.ppermute(
        a, AXES, pairs_of(lambda y, k, x, z: (y + d, k, x, z) if k == 0 else (y, k, x + d, z))
    )


def to_owner(a):
    return lax.ppermute(
        a, AXES, pairs_of(lambda y, k, x, z: (z // 2, z % 2, x, z + 4 * k - y))
    )


SMEM = pl.BlockSpec(memory_space=pltpu.SMEM)
VMEM = pl.BlockSpec(memory_space=pltpu.VMEM)
ANY = pl.BlockSpec(memory_space=pl.ANY)


def call(kernel, out, args, in_specs, out_specs, scratch=(), aliases=None, flops=0, moved=0):
    return pl.pallas_call(
        kernel,
        out_shape=out,
        in_specs=in_specs,
        out_specs=out_specs,
        scratch_shapes=list(scratch),
        input_output_aliases=aliases or {},
        cost_estimate=pl.CostEstimate(flops=flops, bytes_accessed=moved, transcendentals=0),
        compiler_params=pltpu.CompilerParams(vmem_limit_bytes=VMEM_LIMIT),
    )(*args)


def shape(dims, dtype):
    return jax.ShapeDtypeStruct(dims, dtype)


def after_all(value, *others):
    def kernel(*refs):
        pass

    return call(
        kernel,
        shape(value.shape, value.dtype),
        (value, *others),
        [ANY] * (1 + len(others)),
        ANY,
        aliases={0: 0},
    )


def partial_kernel(step, first, *refs):
    place, own_x, other_x, block, other_block = refs[:5]
    keep, one, two, three, token = refs[5:] if first else refs[9:]
    k, p = place[0], place[1]
    slot = jnp.where(k == 0, step, 4 - step)
    token[...] = jnp.zeros_like(token)

    @pl.when((slot >= 0) & (slot < 4))
    def _():
        mine, theirs = block[...].T, other_block[...].T
        for a in range(4):
            at = slice(a * 256, a * 256 + 256)
            tile = jnp.dot(mine, own_x[:, at], preferred_element_type=f32)
            tile = tile + jnp.dot(theirs, other_x[:, at], preferred_element_type=f32)
            d = lax.rem(jnp.where(k == 0, a, slot) - p + 4, 4)
            index = jnp.where(k == 0, slot, a)

            @pl.when(d == 0)
            def _():
                keep[index] = tile

            for m, out in ((1, one), (2, two), (3, three)):

                @pl.when(d == m)
                def _():
                    out[index] = tile.astype(bf16)


def middle_kernel(place, keep, one, two, three, *refs):
    own, s_one, s_two, s_three = refs[3:]
    q = place[2]
    for d, out in enumerate((own, s_one, s_two, s_three)):
        j = lax.rem(q + d, 4)
        out[...] = (
            keep[j] + one[j].astype(f32) + two[j].astype(f32) + three[j].astype(f32)
        )


def adam_kernel(gradient, master, first_moment, second_moment, *outs):
    new_master, new_first, new_second, weight = outs
    gradient = gradient[...].astype(f32).T
    first = beta_one * first_moment[...].astype(f32) + (1.0 - beta_one) * gradient
    second = beta_two * second_moment[...].astype(f32) + (1.0 - beta_two) * gradient * gradient
    corr_one = 1.0 - beta_one**ADAM_STEP
    corr_two = 1.0 - beta_two**ADAM_STEP
    update = first / corr_one / (jnp.sqrt(second / corr_two) + tiny_term)
    update = update + decay_rate * master[...]
    result = master[...] - learn_rate * update
    new_master[...] = result
    new_first[...] = first.astype(bf16)
    new_second[...] = second.astype(bf16)
    weight[...] = result.astype(bf16)


def states_kernel(place, states, kept, sent):
    k, p, q = place[0], place[1], place[2]
    for m in range(4):
        for n in range(4):
            for core, a, b, out in ((k, p, q, kept), (1 - k, q, p, sent)):
                u, v = lax.rem(a + m, 4), lax.rem(b + n, 4)
                x = jnp.where(core == 0, u, v)
                y = jnp.where(core == 0, v, u)
                at = pl.multiple_of(((2 * y + core) * 4 + x) * 256, 256)
                out[m + 4 * n] = states[:, pl.ds(at, 256)]


def project_kernel(base, n, has, kept, came, *refs):
    weights = refs[:n]
    if has:
        before_mine, before_theirs = refs[n : n + 2]
    mine, theirs = refs[-2:]
    total, other = None, None
    if has:
        total, other = before_mine[...], before_theirs[...]
    for i in range(n):
        for m in range(4):
            w = weights[i][m]
            at = base[i] * 4 + m
            term = jnp.dot(kept[at], w, preferred_element_type=f32)
            total = term if total is None else total + term
            term = jnp.dot(came[at], w, preferred_element_type=f32)
            other = term if other is None else other + term
    mine[...] = total
    theirs[...] = other


def finish_kernel(mine, theirs, queries, peak, mass, past, out):
    fresh = (mine[...] + theirs[...]).astype(bf16)
    n = fresh.shape[0]
    rows = n // 4
    group = HEADS // KVH
    line = lax.broadcasted_iota(jnp.int32, (n, n), 0)
    lane = lax.broadcasted_iota(jnp.int32, (n, n), 1)
    seen = (lax.rem(line, rows) == lax.rem(lane, rows)) & (lane <= line)
    seen = jnp.concatenate([seen.astype(f32)] * group, axis=0) > 0.5
    scale = 1.0 / math.sqrt(HD)
    keys, values = fresh[:, :HD], fresh[:, HD:]
    stack = jnp.concatenate([queries[:, g * HD : g * HD + HD] for g in range(group)], axis=0)
    scores = lax.dot_general(
        stack, keys, (((1,), (1,)), ((), ())), preferred_element_type=f32
    )
    scores = jnp.where(seen, scores * scale, -1e30)
    before = jnp.concatenate([peak[:, g : g + 1] for g in range(group)], axis=0)
    mass = jnp.concatenate([mass[:, g : g + 1] for g in range(group)], axis=0)
    top = jnp.maximum(before, jnp.max(scores, axis=1, keepdims=True))
    weight = jnp.where(seen, jnp.exp(scores - top), 0.0)
    fade = jnp.exp(before - top)
    total = mass * fade + jnp.sum(weight, axis=1, keepdims=True)
    probs = (weight / total).astype(bf16)
    result = jnp.dot(probs, values, preferred_element_type=f32)
    result = (result + past[...] * (fade / total)).astype(bf16)
    for g in range(group):
        out[:, g * HD : g * HD + HD] = result[g * n : g * n + n]


def past_part(queries, cache, lengths):
    steps, rows = queries.shape[0], queries.shape[1]
    span = cache.shape[1]
    group = HEADS // KVH
    block = queries.reshape(steps, rows, group, HD)
    scores = jnp.einsum(
        "srgd,rtd->srgt", block, cache[:, :, :HD], preferred_element_type=f32
    ) * (1.0 / math.sqrt(HD))
    live = jnp.arange(span, dtype=jnp.int32)[None, :] < lengths[:, None]
    scores = jnp.where(live[None, :, None, :], scores, -jnp.inf)
    peak = jnp.max(scores, axis=-1)
    weight = jnp.exp(scores - peak[..., None])
    mass = jnp.sum(weight, axis=-1)
    past = jnp.einsum(
        "srgt,rtd->gsrd", weight.astype(bf16), cache[:, :, HD:], preferred_element_type=f32
    )
    n = steps * rows
    return peak.reshape(n, group), mass.reshape(n, group), past.reshape(n * group, HD)


def body(
    train_inputs,
    kv_grads,
    master,
    first_moment,
    second_moment,
    hidden_states,
    queries,
    kv_cache,
    cache_lengths,
):
    f = lax.axis_index("fsdp")
    x = lax.axis_index("rep")
    y, k = f // 2, f % 2
    p = jnp.where(k == 0, x, y)
    q = jnp.where(k == 0, y, x)
    place = jnp.stack([k, p, q]).astype(jnp.int32)
    steps, rows, width = hidden_states.shape
    count = steps * rows

    block = kv_grads
    other_block = swap_core(kv_grads)
    other_x = swap_core(train_inputs)

    part = (4, 256, 256)
    buffers = ()
    outs = (shape(part, f32),) + (shape(part, bf16),) * 3 + (shape((8, 128), f32),)

    def add_slot(step, block, other_block, buffers):
        first = not buffers
        *buffers, token = call(
            functools.partial(partial_kernel, step, first),
            outs,
            (place, train_inputs, other_x, block, other_block, *buffers),
            [SMEM] + [VMEM] * (4 + len(buffers)),
            [VMEM] * 5,
            (),
            {} if first else {5: 0, 6: 1, 7: 2, 8: 3},
            flops=4 * 640 * 1024 * 256,
            moved=6 << 20,
        )
        return tuple(buffers), token

    kept, sent = call(
        states_kernel,
        (shape((16, count, 256), bf16),) * 2,
        (place, hidden_states.reshape(count, width)),
        [SMEM, VMEM],
        [VMEM, VMEM],
        moved=4 << 20,
    )
    tokens = []
    arrived = (block, other_block)
    for step in range(5):
        if step == 1:
            arrived = (arrived[0], after_all(arrived[1], kept))
        if step == 2:
            arrived = (arrived[0], after_all(arrived[1], tokens[0]))
        if step == 3:
            arrived = (arrived[0], after_all(arrived[1], tokens[1]))
        if step < 4:
            after = (pass_on(arrived[0]), pass_on(arrived[1]))
        buffers, token = add_slot(step, *arrived, buffers)
        tokens.append(token)
        arrived = after
    came = swap_core(sent)

    keep, one, two, three = buffers
    peak, mass, past = past_part(queries, kv_cache, cache_lengths)
    one, two, three = shift_first(one, 1), shift_first(two, 2), shift_first(three, 3)
    square = shape((256, 256), f32)
    own, one, two, three = call(
        middle_kernel,
        (square,) * 4,
        (place, keep, one, two, three, past, peak, mass),
        [SMEM] + [VMEM] * 4 + [ANY] * 3,
        [VMEM] * 4,
        moved=4 << 20,
    )
    one, two, three = shift_second(one, 1), shift_second(two, 2), shift_second(three, 3)
    gradient = (own + one + two + three).astype(bf16)
    gradient = to_owner(gradient)
    narrow = shape((256, 256), bf16)
    new_master, new_first, new_second, weight = call(
        adam_kernel,
        (square, narrow, narrow, narrow),
        (gradient, master, first_moment, second_moment),
        [VMEM] * 4,
        [VMEM] * 4,
        moved=1 << 20,
    )

    stack = jnp.stack(
        [weight, shift_first(weight, -1), shift_first(weight, 2), shift_first(weight, 1)]
    )
    ahead, across, behind = shift_second(stack, -1), shift_second(stack, 2), shift_second(stack, 1)
    result = (shape((count, 256), f32),) * 2

    def project(base, weights, before):
        return call(
            functools.partial(project_kernel, base, len(base), bool(before)),
            result,
            (kept, came, *weights, *before),
            [VMEM] * (2 + len(base) + len(before)),
            [VMEM] * 2,
            flops=len(base) * 4 * 4 * 128 * 256 * 256,
            moved=len(base) << 19,
        )

    sums = project((0,), (stack,), ())
    sums = project((1, 3), (ahead, behind), sums)
    mine, theirs = project((2,), (across,), sums)
    got = swap_core(theirs)
    attended = call(
        finish_kernel,
        shape((count, queries.shape[2]), bf16),
        (mine, got, queries.reshape(count, queries.shape[2]), peak, mass, past),
        [VMEM] * 6,
        VMEM,
        moved=1 << 20,
    )
    return new_master, new_first, new_second, attended.reshape(queries.shape)


def solution(mesh):
    in_specs = (
        P(("fsdp", "rep"), "tp"),
        P(("fsdp", "rep"), "tp"),
        P(("fsdp", "rep"), "tp"),
        P(("fsdp", "rep"), "tp"),
        P(("fsdp", "rep"), "tp"),
        P(None, ("fsdp", "rep"), None),
        P(None, ("fsdp", "rep"), "tp"),
        P(("fsdp", "rep"), None, "tp"),
        P(("fsdp", "rep")),
    )
    out_specs = (
        P(("fsdp", "rep"), "tp"),
        P(("fsdp", "rep"), "tp"),
        P(("fsdp", "rep"), "tp"),
        P(None, ("fsdp", "rep"), "tp"),
    )
    return jax.shard_map(body, mesh=mesh, in_specs=in_specs, out_specs=out_specs, check_vma=False)
```

```python
import functools
import math

import jax
import jax.numpy as jnp
from jax import lax
from jax.experimental import pallas as pl
from jax.experimental.pallas import tpu as pltpu
from jax.sharding import PartitionSpec as P

HEADS = 64
KVH = 8
HD = 128
ADAM_STEP = 100

learn_rate = 0.001
beta_one = 0.9
beta_two = 0.95
decay_rate = 0.1
tiny_term = 1e-08

NY, NX, NZ = 4, 4, 8
AXES = ("fsdp", "tp", "rep")
VMEM_LIMIT = 40 * 1024 * 1024
f32 = jnp.float32
bf16 = jnp.bfloat16


def pairs_of(move):
    pairs = []
    for y in range(NY):
        for k in range(2):
            for x in range(NX):
                for z in range(NZ):
                    v, j, u, w = move(y, k, x, z)
                    source = ((y * 2 + k) * NZ + z) * NX + x
                    target = (((v % NY) * 2 + j) * NZ + w % NZ) * NX + u % NX
                    pairs.append((source, target))
    return pairs


def swap_core(a):
    return lax.ppermute(a, AXES, pairs_of(lambda y, k, x, z: (y, 1 - k, x, z)))


def pass_on(a):
    return lax.ppermute(a, AXES, pairs_of(lambda y, k, x, z: (y, k, x, z + 1 - 2 * k)))


def shift_first(a, d):
    return lax.ppermute(
        a, AXES, pairs_of(lambda y, k, x, z: (y, k, x + d, z) if k == 0 else (y + d, k, x, z))
    )


def shift_second(a, d):
    return lax.ppermute(
        a, AXES, pairs_of(lambda y, k, x, z: (y + d, k, x, z) if k == 0 else (y, k, x + d, z))
    )


def to_owner(a):
    return lax.ppermute(
        a, AXES, pairs_of(lambda y, k, x, z: (z // 2, z % 2, x, z + 4 * k - y))
    )


SMEM = pl.BlockSpec(memory_space=pltpu.SMEM)
VMEM = pl.BlockSpec(memory_space=pltpu.VMEM)
ANY = pl.BlockSpec(memory_space=pl.ANY)


def call(kernel, out, args, in_specs, out_specs, scratch=(), aliases=None, flops=0, moved=0):
    return pl.pallas_call(
        kernel,
        out_shape=out,
        in_specs=in_specs,
        out_specs=out_specs,
        scratch_shapes=list(scratch),
        input_output_aliases=aliases or {},
        cost_estimate=pl.CostEstimate(flops=flops, bytes_accessed=moved, transcendentals=0),
        compiler_params=pltpu.CompilerParams(vmem_limit_bytes=VMEM_LIMIT),
    )(*args)


def shape(dims, dtype):
    return jax.ShapeDtypeStruct(dims, dtype)


def after_all(value, *others):
    def kernel(*refs):
        pass

    return call(
        kernel,
        shape(value.shape, value.dtype),
        (value, *others),
        [ANY] * (1 + len(others)),
        ANY,
        aliases={0: 0},
    )


def partial_kernel(step, first, *refs):
    place, own_x, other_x, block, other_block = refs[:5]
    keep, one, two, three, token = refs[5:] if first else refs[9:]
    k, p = place[0], place[1]
    sends = (keep, one, two, three)
    token[...] = jnp.zeros_like(token)

    def tile(mine, theirs, a):
        at = pl.ds(pl.multiple_of(a * 256, 256), 256)
        return jnp.dot(mine, own_x[:, at], preferred_element_type=f32) + jnp.dot(
            theirs, other_x[:, at], preferred_element_type=f32
        )

    if step < 4:

        @pl.when(k == 0)
        def _():
            mine, theirs = block[...].T, other_block[...].T
            for d, out in enumerate(sends):
                out[step] = tile(mine, theirs, lax.rem(p + d, 4)).astype(out.dtype)

    if step > 0:
        slot = 4 - step
        for d, out in enumerate(sends):

            @pl.when((k == 1) & (lax.rem(p + d, 4) == slot))
            def _():
                mine, theirs = block[...].T, other_block[...].T
                for a in range(4):
                    out[a] = tile(mine, theirs, a).astype(out.dtype)


def middle_kernel(place, keep, one, two, three, *refs):
    own, s_one, s_two, s_three = refs[3:]
    q = place[2]
    for d, out in enumerate((own, s_one, s_two, s_three)):
        j = lax.rem(q + d, 4)
        out[...] = (
            keep[j] + one[j].astype(f32) + two[j].astype(f32) + three[j].astype(f32)
        )


def adam_kernel(gradient, master, first_moment, second_moment, *outs):
    new_master, new_first, new_second, weight = outs
    gradient = gradient[...].astype(f32).T
    first = beta_one * first_moment[...].astype(f32) + (1.0 - beta_one) * gradient
    second = beta_two * second_moment[...].astype(f32) + (1.0 - beta_two) * gradient * gradient
    corr_one = 1.0 - beta_one**ADAM_STEP
    corr_two = 1.0 - beta_two**ADAM_STEP
    update = first / corr_one / (jnp.sqrt(second / corr_two) + tiny_term)
    update = update + decay_rate * master[...]
    result = master[...] - learn_rate * update
    new_master[...] = result
    new_first[...] = first.astype(bf16)
    new_second[...] = second.astype(bf16)
    weight[...] = result.astype(bf16)


def states_kernel(place, states, kept, sent):
    k, p, q = place[0], place[1], place[2]
    for m in range(4):
        for n in range(4):
            for core, a, b, out in ((k, p, q, kept), (1 - k, q, p, sent)):
                u, v = lax.rem(a + m, 4), lax.rem(b + n, 4)
                x = jnp.where(core == 0, u, v)
                y = jnp.where(core == 0, v, u)
                at = pl.multiple_of(((2 * y + core) * 4 + x) * 256, 256)
                out[m + 4 * n] = states[:, pl.ds(at, 256)]


def project_kernel(base, n, has, kept, came, *refs):
    weights = refs[:n]
    if has:
        before_mine, before_theirs = refs[n : n + 2]
    mine, theirs = refs[-2:]
    total, other = None, None
    if has:
        total, other = before_mine[...], before_theirs[...]
    for i in range(n):
        for m in range(4):
            w = weights[i][m]
            at = base[i] * 4 + m
            term = jnp.dot(kept[at], w, preferred_element_type=f32)
            total = term if total is None else total + term
            term = jnp.dot(came[at], w, preferred_element_type=f32)
            other = term if other is None else other + term
    mine[...] = total
    theirs[...] = other


def finish_kernel(mine, theirs, queries, peak, mass, past, out):
    fresh = (mine[...] + theirs[...]).astype(bf16)
    n = fresh.shape[0]
    rows = n // 4
    group = HEADS // KVH
    line = lax.broadcasted_iota(jnp.int32, (n, n), 0)
    lane = lax.broadcasted_iota(jnp.int32, (n, n), 1)
    seen = (lax.rem(line, rows) == lax.rem(lane, rows)) & (lane <= line)
    seen = jnp.concatenate([seen.astype(f32)] * group, axis=0) > 0.5
    scale = 1.0 / math.sqrt(HD)
    keys, values = fresh[:, :HD], fresh[:, HD:]
    stack = jnp.concatenate([queries[:, g * HD : g * HD + HD] for g in range(group)], axis=0)
    scores = lax.dot_general(
        stack, keys, (((1,), (1,)), ((), ())), preferred_element_type=f32
    )
    scores = jnp.where(seen, scores * scale, -1e30)
    before = jnp.concatenate([peak[:, g : g + 1] for g in range(group)], axis=0)
    mass = jnp.concatenate([mass[:, g : g + 1] for g in range(group)], axis=0)
    top = jnp.maximum(before, jnp.max(scores, axis=1, keepdims=True))
    weight = jnp.where(seen, jnp.exp(scores - top), 0.0)
    fade = jnp.exp(before - top)
    total = mass * fade + jnp.sum(weight, axis=1, keepdims=True)
    probs = (weight / total).astype(bf16)
    result = jnp.dot(probs, values, preferred_element_type=f32)
    result = (result + past[...] * (fade / total)).astype(bf16)
    for g in range(group):
        out[:, g * HD : g * HD + HD] = result[g * n : g * n + n]


def past_part(queries, cache, lengths):
    steps, rows = queries.shape[0], queries.shape[1]
    span = cache.shape[1]
    group = HEADS // KVH
    block = queries.reshape(steps, rows, group, HD)
    scores = jnp.einsum(
        "srgd,rtd->srgt", block, cache[:, :, :HD], preferred_element_type=f32
    ) * (1.0 / math.sqrt(HD))
    live = jnp.arange(span, dtype=jnp.int32)[None, :] < lengths[:, None]
    scores = jnp.where(live[None, :, None, :], scores, -jnp.inf)
    peak = jnp.max(scores, axis=-1)
    weight = jnp.exp(scores - peak[..., None])
    mass = jnp.sum(weight, axis=-1)
    past = jnp.einsum(
        "srgt,rtd->gsrd", weight.astype(bf16), cache[:, :, HD:], preferred_element_type=f32
    )
    n = steps * rows
    return peak.reshape(n, group), mass.reshape(n, group), past.reshape(n * group, HD)


def body(
    train_inputs,
    kv_grads,
    master,
    first_moment,
    second_moment,
    hidden_states,
    queries,
    kv_cache,
    cache_lengths,
):
    f = lax.axis_index("fsdp")
    x = lax.axis_index("rep")
    y, k = f // 2, f % 2
    p = jnp.where(k == 0, x, y)
    q = jnp.where(k == 0, y, x)
    place = jnp.stack([k, p, q]).astype(jnp.int32)
    steps, rows, width = hidden_states.shape
    count = steps * rows

    block = kv_grads
    other_block = swap_core(kv_grads)
    other_x = swap_core(train_inputs)

    part = (4, 256, 256)
    buffers = ()
    outs = (shape(part, f32),) + (shape(part, bf16),) * 3 + (shape((8, 128), f32),)

    def add_slot(step, block, other_block, buffers):
        first = not buffers
        *buffers, token = call(
            functools.partial(partial_kernel, step, first),
            outs,
            (place, train_inputs, other_x, block, other_block, *buffers),
            [SMEM] + [VMEM] * (4 + len(buffers)),
            [VMEM] * 5,
            (),
            {} if first else {5: 0, 6: 1, 7: 2, 8: 3},
            flops=4 * 640 * 1024 * 256,
            moved=6 << 20,
        )
        return tuple(buffers), token

    kept, sent = call(
        states_kernel,
        (shape((16, count, 256), bf16),) * 2,
        (place, hidden_states.reshape(count, width)),
        [SMEM, VMEM],
        [VMEM, VMEM],
        moved=4 << 20,
    )
    tokens = []
    arrived = (block, other_block)
    for step in range(5):
        if 0 < step < 4:
            awaited = (tokens[-1], kept) if step == 1 else (tokens[-1],)
            arrived = (arrived[0], after_all(arrived[1], *awaited))
        if step < 4:
            after = (pass_on(arrived[0]), pass_on(arrived[1]))
        buffers, token = add_slot(step, *arrived, buffers)
        tokens.append(token)
        arrived = after
    came = swap_core(sent)

    keep, one, two, three = buffers
    peak, mass, past = past_part(queries, kv_cache, cache_lengths)
    one, two, three = shift_first(one, 1), shift_first(two, 2), shift_first(three, 3)
    square = shape((256, 256), f32)
    own, one, two, three = call(
        middle_kernel,
        (square,) * 4,
        (place, keep, one, two, three, past, peak, mass),
        [SMEM] + [VMEM] * 4 + [ANY] * 3,
        [VMEM] * 4,
        moved=4 << 20,
    )
    one, two, three = shift_second(one, 1), shift_second(two, 2), shift_second(three, 3)
    gradient = (own + one + two + three).astype(bf16)
    gradient = to_owner(gradient)
    narrow = shape((256, 256), bf16)
    new_master, new_first, new_second, weight = call(
        adam_kernel,
        (square, narrow, narrow, narrow),
        (gradient, master, first_moment, second_moment),
        [VMEM] * 4,
        [VMEM] * 4,
        moved=1 << 20,
    )

    stack = jnp.stack(
        [weight, shift_first(weight, -1), shift_first(weight, 2), shift_first(weight, 1)]
    )
    ahead, across, behind = shift_second(stack, -1), shift_second(stack, 2), shift_second(stack, 1)
    result = (shape((count, 256), f32),) * 2

    def project(base, weights, before):
        return call(
            functools.partial(project_kernel, base, len(base), bool(before)),
            result,
            (kept, came, *weights, *before),
            [VMEM] * (2 + len(base) + len(before)),
            [VMEM] * 2,
            flops=len(base) * 4 * 4 * 128 * 256 * 256,
            moved=len(base) << 19,
        )

    sums = project((0,), (stack,), ())
    sums = project((1, 3), (ahead, behind), sums)
    mine, theirs = project((2,), (across,), sums)
    got = swap_core(theirs)
    attended = call(
        finish_kernel,
        shape((count, queries.shape[2]), bf16),
        (mine, got, queries.reshape(count, queries.shape[2]), peak, mass, past),
        [VMEM] * 6,
        VMEM,
        moved=1 << 20,
    )
    return new_master, new_first, new_second, attended.reshape(queries.shape)


def solution(mesh):
    in_specs = (
        P(("fsdp", "rep"), "tp"),
        P(("fsdp", "rep"), "tp"),
        P(("fsdp", "rep"), "tp"),
        P(("fsdp", "rep"), "tp"),
        P(("fsdp", "rep"), "tp"),
        P(None, ("fsdp", "rep"), None),
        P(None, ("fsdp", "rep"), "tp"),
        P(("fsdp", "rep"), None, "tp"),
        P(("fsdp", "rep")),
    )
    out_specs = (
        P(("fsdp", "rep"), "tp"),
        P(("fsdp", "rep"), "tp"),
        P(("fsdp", "rep"), "tp"),
        P(None, ("fsdp", "rep"), "tp"),
    )
    return jax.shard_map(body, mesh=mesh, in_specs=in_specs, out_specs=out_specs, check_vma=False)
```

```python
import functools
import math

import jax
import jax.numpy as jnp
from jax import lax
from jax.experimental import pallas as pl
from jax.experimental.pallas import tpu as pltpu
from jax.sharding import PartitionSpec as P

HEADS = 64
KVH = 8
HD = 128
ADAM_STEP = 100

learn_rate = 0.001
beta_one = 0.9
beta_two = 0.95
decay_rate = 0.1
tiny_term = 1e-08

NY, NX, NZ = 4, 4, 8
AXES = ("fsdp", "tp", "rep")
VMEM_LIMIT = 40 * 1024 * 1024
f32 = jnp.float32
bf16 = jnp.bfloat16


def pairs_of(move):
    pairs = []
    for y in range(NY):
        for k in range(2):
            for x in range(NX):
                for z in range(NZ):
                    v, j, u, w = move(y, k, x, z)
                    source = ((y * 2 + k) * NZ + z) * NX + x
                    target = (((v % NY) * 2 + j) * NZ + w % NZ) * NX + u % NX
                    pairs.append((source, target))
    return pairs


def swap_core(a):
    return lax.ppermute(a, AXES, pairs_of(lambda y, k, x, z: (y, 1 - k, x, z)))


def pass_on(a):
    return lax.ppermute(a, AXES, pairs_of(lambda y, k, x, z: (y, k, x, z + 1 - 2 * k)))


def shift_first(a, d):
    return lax.ppermute(
        a, AXES, pairs_of(lambda y, k, x, z: (y, k, x + d, z) if k == 0 else (y + d, k, x, z))
    )


def shift_second(a, d):
    return lax.ppermute(
        a, AXES, pairs_of(lambda y, k, x, z: (y + d, k, x, z) if k == 0 else (y, k, x + d, z))
    )


def to_owner(a):
    return lax.ppermute(
        a, AXES, pairs_of(lambda y, k, x, z: (z // 2, z % 2, x, z + 4 * k - y))
    )


SMEM = pl.BlockSpec(memory_space=pltpu.SMEM)
VMEM = pl.BlockSpec(memory_space=pltpu.VMEM)
ANY = pl.BlockSpec(memory_space=pl.ANY)


def call(kernel, out, args, in_specs, out_specs, scratch=(), aliases=None, flops=0, moved=0):
    return pl.pallas_call(
        kernel,
        out_shape=out,
        in_specs=in_specs,
        out_specs=out_specs,
        scratch_shapes=list(scratch),
        input_output_aliases=aliases or {},
        cost_estimate=pl.CostEstimate(flops=flops, bytes_accessed=moved, transcendentals=0),
        compiler_params=pltpu.CompilerParams(vmem_limit_bytes=VMEM_LIMIT),
    )(*args)


def shape(dims, dtype):
    return jax.ShapeDtypeStruct(dims, dtype)


def after_all(value, *others):
    def kernel(*refs):
        pass

    return call(
        kernel,
        shape(value.shape, value.dtype),
        (value, *others),
        [ANY] * (1 + len(others)),
        ANY,
        aliases={0: 0},
    )


def partial_kernel(step, first, *refs):
    place, own_x, other_x, block, other_block = refs[:5]
    keep, one, two, three, token = refs[5:] if first else refs[9:]
    k, p = place[0], place[1]
    sends = (keep, one, two, three)
    token[...] = jnp.zeros_like(token)

    def tile(mine, theirs, a):
        at = pl.ds(pl.multiple_of(a * 256, 256), 256)
        return jnp.dot(mine, own_x[:, at], preferred_element_type=f32) + jnp.dot(
            theirs, other_x[:, at], preferred_element_type=f32
        )

    if step < 4:

        @pl.when(k == 0)
        def _():
            mine, theirs = block[...].T, other_block[...].T
            for d, out in enumerate(sends):
                out[step] = tile(mine, theirs, lax.rem(p + d, 4)).astype(out.dtype)

    if step > 0:
        slot = 4 - step
        for d, out in enumerate(sends):

            @pl.when((k == 1) & (lax.rem(p + d, 4) == slot))
            def _():
                mine, theirs = block[...].T, other_block[...].T
                for a in range(4):
                    out[a] = tile(mine, theirs, a).astype(out.dtype)


def middle_kernel(place, keep, one, two, three, *refs):
    own, s_one, s_two, s_three = refs[6:]
    q = place[2]
    for d, out in enumerate((own, s_one, s_two, s_three)):
        j = lax.rem(q + d, 4)
        out[...] = (
            keep[j] + one[j].astype(f32) + two[j].astype(f32) + three[j].astype(f32)
        )


def adam_kernel(gradient, master, first_moment, second_moment, *outs):
    new_master, new_first, new_second, weight = outs
    gradient = gradient[...].astype(f32).T
    first = beta_one * first_moment[...].astype(f32) + (1.0 - beta_one) * gradient
    second = beta_two * second_moment[...].astype(f32) + (1.0 - beta_two) * gradient * gradient
    corr_one = 1.0 - beta_one**ADAM_STEP
    corr_two = 1.0 - beta_two**ADAM_STEP
    update = first / corr_one / (jnp.sqrt(second / corr_two) + tiny_term)
    update = update + decay_rate * master[...]
    result = master[...] - learn_rate * update
    new_master[...] = result
    new_first[...] = first.astype(bf16)
    new_second[...] = second.astype(bf16)
    weight[...] = result.astype(bf16)


def states_kernel(place, states, *sends):
    k, p, q = place[0], place[1], place[2]
    for m in range(4):
        for n in range(4):
            u, v = lax.rem(p + m, 4), lax.rem(q + n, 4)
            x = jnp.where(k == 0, u, v)
            y = jnp.where(k == 0, v, u)
            for i, core in enumerate((k, 1 - k)):
                at = pl.multiple_of(((2 * y + core) * 4 + x) * 256, 256)
                sends[m][n, i] = states[:, pl.ds(at, 256)]


def regroup_kernel(*refs):
    came, sends, token = refs[:4], refs[4:8], refs[8]
    token[...] = jnp.zeros_like(token)
    for n in range(4):
        for m in range(4):
            sends[n][m] = came[m][n]


def project_kernel(weight, other_weight, *refs):
    states, sends = refs[:4], refs[4:]
    for m, out in enumerate(sends):
        for n in range(4):
            term = jnp.dot(states[n][m, 0], weight[...], preferred_element_type=f32)
            term = term + jnp.dot(states[n][m, 1], other_weight[...], preferred_element_type=f32)
            out[n] = term.astype(out.dtype)


def gather_kernel(keep, one, two, three, *outs):
    for n, out in enumerate(outs):
        out[...] = (
            keep[n] + one[n].astype(f32) + two[n].astype(f32) + three[n].astype(f32)
        )


def finish_kernel(own, one, two, three, queries, peak, mass, past, out):
    fresh = (own[...] + one[...] + two[...] + three[...]).astype(bf16)
    n = fresh.shape[0]
    rows = n // 4
    group = HEADS // KVH
    line = lax.broadcasted_iota(jnp.int32, (n, n), 0)
    lane = lax.broadcasted_iota(jnp.int32, (n, n), 1)
    seen = (lax.rem(line, rows) == lax.rem(lane, rows)) & (lane <= line)
    seen = jnp.concatenate([seen.astype(f32)] * group, axis=0) > 0.5
    scale = 1.0 / math.sqrt(HD)
    keys, values = fresh[:, :HD], fresh[:, HD:]
    stack = jnp.concatenate([queries[:, g * HD : g * HD + HD] for g in range(group)], axis=0)
    scores = lax.dot_general(
        stack, keys, (((1,), (1,)), ((), ())), preferred_element_type=f32
    )
    scores = jnp.where(seen, scores * scale, -1e30)
    before = jnp.concatenate([peak[:, g : g + 1] for g in range(group)], axis=0)
    mass = jnp.concatenate([mass[:, g : g + 1] for g in range(group)], axis=0)
    top = jnp.maximum(before, jnp.max(scores, axis=1, keepdims=True))
    weight = jnp.where(seen, jnp.exp(scores - top), 0.0)
    fade = jnp.exp(before - top)
    total = mass * fade + jnp.sum(weight, axis=1, keepdims=True)
    probs = (weight / total).astype(bf16)
    result = jnp.dot(probs, values, preferred_element_type=f32)
    result = (result + past[...] * (fade / total)).astype(bf16)
    for g in range(group):
        out[:, g * HD : g * HD + HD] = result[g * n : g * n + n]


def past_part(queries, cache, lengths):
    steps, rows = queries.shape[0], queries.shape[1]
    span = cache.shape[1]
    group = HEADS // KVH
    block = queries.reshape(steps, rows, group, HD)
    scores = jnp.einsum(
        "srgd,rtd->srgt", block, cache[:, :, :HD], preferred_element_type=f32
    ) * (1.0 / math.sqrt(HD))
    live = jnp.arange(span, dtype=jnp.int32)[None, :] < lengths[:, None]
    scores = jnp.where(live[None, :, None, :], scores, -jnp.inf)
    peak = jnp.max(scores, axis=-1)
    weight = jnp.exp(scores - peak[..., None])
    mass = jnp.sum(weight, axis=-1)
    past = jnp.einsum(
        "srgt,rtd->gsrd", weight.astype(bf16), cache[:, :, HD:], preferred_element_type=f32
    )
    n = steps * rows
    return peak.reshape(n, group), mass.reshape(n, group), past.reshape(n * group, HD)


def body(
    train_inputs,
    kv_grads,
    master,
    first_moment,
    second_moment,
    hidden_states,
    queries,
    kv_cache,
    cache_lengths,
):
    f = lax.axis_index("fsdp")
    x = lax.axis_index("rep")
    y, k = f // 2, f % 2
    p = jnp.where(k == 0, x, y)
    q = jnp.where(k == 0, y, x)
    place = jnp.stack([k, p, q]).astype(jnp.int32)
    steps, rows, width = hidden_states.shape
    count = steps * rows

    block = kv_grads
    other_block = swap_core(kv_grads)
    other_x = swap_core(train_inputs)

    part = (4, 256, 256)
    buffers = ()
    outs = (shape(part, f32),) + (shape(part, bf16),) * 3 + (shape((8, 128), f32),)

    def add_slot(step, block, other_block, buffers):
        first = not buffers
        *buffers, token = call(
            functools.partial(partial_kernel, step, first),
            outs,
            (place, train_inputs, other_x, block, other_block, *buffers),
            [SMEM] + [VMEM] * (4 + len(buffers)),
            [VMEM] * 5,
            (),
            {} if first else {5: 0, 6: 1, 7: 2, 8: 3},
            flops=4 * 640 * 1024 * 256,
            moved=6 << 20,
        )
        return tuple(buffers), token

    group = (4, 2, count, 256)
    sends = call(
        states_kernel,
        (shape(group, bf16),) * 4,
        (place, hidden_states.reshape(count, width)),
        [SMEM, VMEM],
        [VMEM] * 4,
        moved=4 << 20,
    )
    came = [sends[0]] + [shift_first(sends[d], d) for d in (1, 2, 3)]
    *sends, regrouped = call(
        regroup_kernel,
        (shape(group, bf16),) * 4 + (shape((8, 128), f32),),
        tuple(came),
        [VMEM] * 4,
        [VMEM] * 5,
        moved=4 << 20,
    )
    states = [sends[0]] + [shift_second(sends[d], d) for d in (1, 2, 3)]

    tokens = []
    arrived = (block, other_block)
    for step in range(5):
        if 0 < step < 4:
            awaited = (tokens[-1], regrouped) if step == 3 else (tokens[-1],)
            arrived = (arrived[0], after_all(arrived[1], *awaited))
        if step < 4:
            after = (pass_on(arrived[0]), pass_on(arrived[1]))
        buffers, token = add_slot(step, *arrived, buffers)
        tokens.append(token)
        arrived = after

    keep, one, two, three = buffers
    peak, mass, past = past_part(queries, kv_cache, cache_lengths)
    one, two, three = shift_first(one, 1), shift_first(two, 2), shift_first(three, 3)
    square = shape((256, 256), f32)
    own, one, two, three = call(
        middle_kernel,
        (square,) * 4,
        (place, keep, one, two, three, past, peak, mass, *states[1:]),
        [SMEM] + [VMEM] * 4 + [ANY] * 6,
        [VMEM] * 4,
        moved=4 << 20,
    )
    one, two, three = shift_second(one, 1), shift_second(two, 2), shift_second(three, 3)
    gradient = (own + one + two + three).astype(bf16)
    gradient = to_owner(gradient)
    narrow = shape((256, 256), bf16)
    new_master, new_first, new_second, weight = call(
        adam_kernel,
        (square, narrow, narrow, narrow),
        (gradient, master, first_moment, second_moment),
        [VMEM] * 4,
        [VMEM] * 4,
        moved=1 << 20,
    )

    part = (4, count, 256)
    keep, one, two, three = call(
        project_kernel,
        (shape(part, f32),) + (shape(part, bf16),) * 3,
        (weight, swap_core(weight), *states),
        [VMEM] * 6,
        [VMEM] * 4,
        flops=2 * 16 * count * 512 * 256,
        moved=4 << 20,
    )
    one, two, three = shift_first(one, -1), shift_first(two, -2), shift_first(three, -3)
    result = shape((count, 256), f32)
    own, one, two, three = call(
        gather_kernel,
        (result,) * 4,
        (keep, one, two, three),
        [VMEM] * 4,
        [VMEM] * 4,
        moved=2 << 20,
    )
    one, two, three = shift_second(one, -1), shift_second(two, -2), shift_second(three, -3)
    attended = call(
        finish_kernel,
        shape((count, queries.shape[2]), bf16),
        (own, one, two, three, queries.reshape(count, queries.shape[2]), peak, mass, past),
        [VMEM] * 8,
        VMEM,
        moved=1 << 20,
    )
    return new_master, new_first, new_second, attended.reshape(queries.shape)


def solution(mesh):
    in_specs = (
        P(("fsdp", "rep"), "tp"),
        P(("fsdp", "rep"), "tp"),
        P(("fsdp", "rep"), "tp"),
        P(("fsdp", "rep"), "tp"),
        P(("fsdp", "rep"), "tp"),
        P(None, ("fsdp", "rep"), None),
        P(None, ("fsdp", "rep"), "tp"),
        P(("fsdp", "rep"), None, "tp"),
        P(("fsdp", "rep")),
    )
    out_specs = (
        P(("fsdp", "rep"), "tp"),
        P(("fsdp", "rep"), "tp"),
        P(("fsdp", "rep"), "tp"),
        P(None, ("fsdp", "rep"), "tp"),
    )
    return jax.shard_map(body, mesh=mesh, in_specs=in_specs, out_specs=out_specs, check_vma=False)
```

```python
import functools
import math

import jax
import jax.numpy as jnp
from jax import lax
from jax.experimental import pallas as pl
from jax.experimental.pallas import tpu as pltpu
from jax.sharding import PartitionSpec as P

HEADS = 64
KVH = 8
HD = 128
ADAM_STEP = 100

learn_rate = 0.001
beta_one = 0.9
beta_two = 0.95
decay_rate = 0.1
tiny_term = 1e-08

NY, NX, NZ = 4, 4, 8
AXES = ("fsdp", "tp", "rep")
VMEM_LIMIT = 40 * 1024 * 1024
f32 = jnp.float32
bf16 = jnp.bfloat16


def pairs_of(move):
    pairs = []
    for y in range(NY):
        for k in range(2):
            for x in range(NX):
                for z in range(NZ):
                    v, j, u, w = move(y, k, x, z)
                    source = ((y * 2 + k) * NZ + z) * NX + x
                    target = (((v % NY) * 2 + j) * NZ + w % NZ) * NX + u % NX
                    pairs.append((source, target))
    return pairs


def swap_core(a):
    return lax.ppermute(a, AXES, pairs_of(lambda y, k, x, z: (y, 1 - k, x, z)))


def pass_on(a):
    return lax.ppermute(a, AXES, pairs_of(lambda y, k, x, z: (y, k, x, z + 1 - 2 * k)))


def pass_last(a):
    pairs = pairs_of(lambda y, k, x, z: (y, k, x, z - 1))
    return lax.ppermute(a, AXES, [m for m in pairs if m[0] // (NX * NZ) % 2 == 1])


def shift_first(a, d):
    return lax.ppermute(
        a, AXES, pairs_of(lambda y, k, x, z: (y, k, x + d, z) if k == 0 else (y + d, k, x, z))
    )


def shift_second(a, d):
    return lax.ppermute(
        a, AXES, pairs_of(lambda y, k, x, z: (y + d, k, x, z) if k == 0 else (y, k, x + d, z))
    )


def to_owner(a):
    return lax.ppermute(
        a, AXES, pairs_of(lambda y, k, x, z: (z // 2, z % 2, x, z + 4 * k - y))
    )


SMEM = pl.BlockSpec(memory_space=pltpu.SMEM)
VMEM = pl.BlockSpec(memory_space=pltpu.VMEM)
ANY = pl.BlockSpec(memory_space=pl.ANY)


def call(kernel, out, args, in_specs, out_specs, scratch=(), aliases=None, flops=0, moved=0):
    return pl.pallas_call(
        kernel,
        out_shape=out,
        in_specs=in_specs,
        out_specs=out_specs,
        scratch_shapes=list(scratch),
        input_output_aliases=aliases or {},
        cost_estimate=pl.CostEstimate(flops=flops, bytes_accessed=moved, transcendentals=0),
        compiler_params=pltpu.CompilerParams(vmem_limit_bytes=VMEM_LIMIT),
    )(*args)


def shape(dims, dtype):
    return jax.ShapeDtypeStruct(dims, dtype)


def after_all(value, *others):
    def kernel(*refs):
        pass

    return call(
        kernel,
        shape(value.shape, value.dtype),
        (value, *others),
        [ANY] * (1 + len(others)),
        ANY,
        aliases={0: 0},
    )


def partial_kernel(step, *refs):
    place, own_x, other_x, block, other_block = refs[:5]
    keep, one, two, three, token, turned = refs[-6:]
    k, p = place[0], place[1]
    slot = jnp.where(k == 0, step, 4 - step)
    token[...] = jnp.zeros_like(token)

    @pl.when((slot >= 0) & (slot < 4))
    def _():
        turned[0] = block[...].T
        turned[1] = other_block[...].T

        def one_tile(i, carry):
            a = jnp.where(k == 0, lax.rem(p + i, 4), i)
            d = jnp.where(k == 0, i, lax.rem(slot - p + 4, 4))
            index = jnp.where(k == 0, slot, i)
            at = pl.ds(pl.multiple_of(a * 256, 256), 256)
            tile = jnp.dot(turned[0], own_x[:, at], preferred_element_type=f32)
            tile = tile + jnp.dot(turned[1], other_x[:, at], preferred_element_type=f32)

            @pl.when(d == 0)
            def _():
                keep[index] = tile

            for m, out in ((1, one), (2, two), (3, three)):

                @pl.when(d == m)
                def _():
                    out[index] = tile.astype(bf16)

            return carry

        lax.fori_loop(0, 4, one_tile, 0)


def middle_kernel(place, keep, one, two, three, *refs):
    own, s_one, s_two, s_three = refs[3:]
    q = place[2]
    for d, out in enumerate((own, s_one, s_two, s_three)):
        j = lax.rem(q + d, 4)
        out[...] = (
            keep[j] + one[j].astype(f32) + two[j].astype(f32) + three[j].astype(f32)
        ).astype(out.dtype)


def adam_kernel(gradient, master, first_moment, second_moment, *outs):
    new_master, new_first, new_second, weight = outs
    gradient = gradient[...].astype(f32).T
    first = beta_one * first_moment[...].astype(f32) + (1.0 - beta_one) * gradient
    second = beta_two * second_moment[...].astype(f32) + (1.0 - beta_two) * gradient * gradient
    corr_one = 1.0 - beta_one**ADAM_STEP
    corr_two = 1.0 - beta_two**ADAM_STEP
    update = first / corr_one / (jnp.sqrt(second / corr_two) + tiny_term)
    update = update + decay_rate * master[...]
    result = master[...] - learn_rate * update
    new_master[...] = result
    new_first[...] = first.astype(bf16)
    new_second[...] = second.astype(bf16)
    weight[...] = result.astype(bf16)


def states_kernel(place, states, *refs):
    sends, token, sems = refs[:4], refs[4], refs[5]
    k, p, q = place[0], place[1], place[2]
    copies = []
    for m in range(4):
        for n in range(4):
            u, v = lax.rem(p + m, 4), lax.rem(q + n, 4)
            x = jnp.where(k == 0, u, v)
            y = jnp.where(k == 0, v, u)
            for i, core in enumerate((k, 1 - k)):
                at = pl.multiple_of(((2 * y + core) * 4 + x) * 256, 256)
                copies.append(
                    pltpu.make_async_copy(
                        states.at[:, pl.ds(at, 256)], sends[m].at[n, i], sems.at[len(copies)]
                    )
                )
                copies[-1].start()
    token[...] = jnp.zeros_like(token)
    for copy in copies:
        copy.wait()


def regroup_kernel(*refs):
    came, sends, token = refs[:4], refs[4:8], refs[8]
    token[...] = jnp.zeros_like(token)
    for n in range(4):
        for m in range(4):
            sends[n][m] = came[m][n]


def project_kernel(weight, other_weight, *refs):
    states, sends = refs[:4], refs[4:]
    for m, out in enumerate(sends):
        for n in range(4):
            term = jnp.dot(states[n][m, 0], weight[...], preferred_element_type=f32)
            term = term + jnp.dot(states[n][m, 1], other_weight[...], preferred_element_type=f32)
            out[n] = term.astype(out.dtype)


def gather_kernel(keep, one, two, three, *outs):
    for n, out in enumerate(outs):
        out[...] = (
            keep[n] + one[n].astype(f32) + two[n].astype(f32) + three[n].astype(f32)
        )


def finish_kernel(own, one, two, three, queries, peak, mass, past, out):
    fresh = (own[...] + one[...] + two[...] + three[...]).astype(bf16)
    n = fresh.shape[0]
    rows = n // 4
    group = HEADS // KVH
    line = lax.broadcasted_iota(jnp.int32, (n, n), 0)
    lane = lax.broadcasted_iota(jnp.int32, (n, n), 1)
    seen = (lax.rem(line, rows) == lax.rem(lane, rows)) & (lane <= line)
    seen = jnp.concatenate([seen.astype(f32)] * group, axis=0) > 0.5
    scale = 1.0 / math.sqrt(HD)
    keys, values = fresh[:, :HD], fresh[:, HD:]
    stack = jnp.concatenate([queries[:, g * HD : g * HD + HD] for g in range(group)], axis=0)
    scores = lax.dot_general(
        stack, keys, (((1,), (1,)), ((), ())), preferred_element_type=f32
    )
    scores = jnp.where(seen, scores * scale, -1e30)
    before = jnp.concatenate([peak[:, g : g + 1] for g in range(group)], axis=0)
    mass = jnp.concatenate([mass[:, g : g + 1] for g in range(group)], axis=0)
    top = jnp.maximum(before, jnp.max(scores, axis=1, keepdims=True))
    weight = jnp.where(seen, jnp.exp(scores - top), 0.0)
    fade = jnp.exp(before - top)
    total = mass * fade + jnp.sum(weight, axis=1, keepdims=True)
    probs = (weight / total).astype(bf16)
    result = jnp.dot(probs, values, preferred_element_type=f32)
    result = (result + past[...] * (fade / total)).astype(bf16)
    for g in range(group):
        out[:, g * HD : g * HD + HD] = result[g * n : g * n + n]


def past_part(queries, cache, lengths):
    steps, rows = queries.shape[0], queries.shape[1]
    span = cache.shape[1]
    group = HEADS // KVH
    block = queries.reshape(steps, rows, group, HD)
    scores = jnp.einsum(
        "srgd,rtd->srgt", block, cache[:, :, :HD], preferred_element_type=f32
    ) * (1.0 / math.sqrt(HD))
    live = jnp.arange(span, dtype=jnp.int32)[None, :] < lengths[:, None]
    scores = jnp.where(live[None, :, None, :], scores, -jnp.inf)
    peak = jnp.max(scores, axis=-1)
    weight = jnp.exp(scores - peak[..., None])
    mass = jnp.sum(weight, axis=-1)
    past = jnp.einsum(
        "srgt,rtd->gsrd", weight.astype(bf16), cache[:, :, HD:], preferred_element_type=f32
    )
    n = steps * rows
    return peak.reshape(n, group), mass.reshape(n, group), past.reshape(n * group, HD)


def body(
    train_inputs,
    kv_grads,
    master,
    first_moment,
    second_moment,
    hidden_states,
    queries,
    kv_cache,
    cache_lengths,
):
    f = lax.axis_index("fsdp")
    x = lax.axis_index("rep")
    y, k = f // 2, f % 2
    p = jnp.where(k == 0, x, y)
    q = jnp.where(k == 0, y, x)
    place = jnp.stack([k, p, q]).astype(jnp.int32)
    steps, rows, width = hidden_states.shape
    count = steps * rows

    block = kv_grads
    other_block = swap_core(kv_grads)
    other_x = swap_core(train_inputs)

    part = (4, 256, 256)
    buffers = ()
    outs = (shape(part, f32),) + (shape(part, bf16),) * 3 + (shape((8, 128), f32),)

    def add_slot(step, block, other_block, buffers, awaited=()):
        first = not buffers
        *buffers, token = call(
            functools.partial(partial_kernel, step),
            outs,
            (place, train_inputs, other_x, block, other_block, *buffers, *awaited),
            [SMEM] + [VMEM] * (4 + len(buffers)) + [ANY] * len(awaited),
            [VMEM] * 5,
            [pltpu.VMEM((2, 256, 640), bf16)],
            {} if first else {5: 0, 6: 1, 7: 2, 8: 3},
            flops=4 * 640 * 1024 * 256,
            moved=6 << 20,
        )
        return tuple(buffers), token

    group = (4, 2, count, 256)
    *sends, packed = call(
        states_kernel,
        (shape(group, bf16),) * 4 + (shape((8, 128), f32),),
        (place, hidden_states.reshape(count, width)),
        [SMEM, pl.BlockSpec(memory_space=pltpu.HBM)],
        [VMEM] * 5,
        [pltpu.SemaphoreType.DMA((32,))],
        moved=4 << 20,
    )
    other_block = after_all(other_block, packed)
    came = [sends[0]] + [shift_first(sends[d], d) for d in (1, 2, 3)]
    *sends, regrouped = call(
        regroup_kernel,
        (shape(group, bf16),) * 4 + (shape((8, 128), f32),),
        tuple(came),
        [VMEM] * 4,
        [VMEM] * 5,
        moved=4 << 20,
    )
    states = [sends[0]] + [shift_second(sends[d], d) for d in (1, 2, 3)]

    tokens = []
    arrived = (block, other_block)
    for step in range(5):
        if 0 < step < 4:
            awaited = (tokens[-1], regrouped) if step == 3 else (tokens[-1],)
            arrived = (arrived[0], after_all(arrived[1], *awaited))
        if step < 4:
            send = pass_on if step < 3 else pass_last
            after = (send(arrived[0]), send(arrived[1]))
        buffers, token = add_slot(step, *arrived, buffers)
        tokens.append(token)
        arrived = after

    keep, one, two, three = buffers
    peak, mass, past = past_part(queries, kv_cache, cache_lengths)
    two = after_all(two, *states[1:])
    one, two, three = shift_first(one, 1), shift_first(two, 2), shift_first(three, 3)
    square, narrow = shape((256, 256), f32), shape((256, 256), bf16)
    own, one, two, three = call(
        middle_kernel,
        (square, narrow, narrow, narrow),
        (place, keep, one, two, three, past, peak, mass),
        [SMEM] + [VMEM] * 4 + [ANY] * 3,
        [VMEM] * 4,
        moved=4 << 20,
    )
    one, two, three = shift_second(one, 1), shift_second(two, 2), shift_second(three, 3)
    gradient = own + one.astype(f32) + two.astype(f32) + three.astype(f32)
    gradient = gradient.astype(bf16)
    gradient = to_owner(gradient)
    new_master, new_first, new_second, weight = call(
        adam_kernel,
        (square, narrow, narrow, narrow),
        (gradient, master, first_moment, second_moment),
        [VMEM] * 4,
        [VMEM] * 4,
        moved=1 << 20,
    )

    part = (4, count, 256)
    keep, one, two, three = call(
        project_kernel,
        (shape(part, f32),) + (shape(part, bf16),) * 3,
        (weight, swap_core(weight), *states),
        [VMEM] * 6,
        [VMEM] * 4,
        flops=2 * 16 * count * 512 * 256,
        moved=4 << 20,
    )
    one, two, three = shift_first(one, -1), shift_first(two, -2), shift_first(three, -3)
    result = shape((count, 256), f32)
    own, one, two, three = call(
        gather_kernel,
        (result,) * 4,
        (keep, one, two, three),
        [VMEM] * 4,
        [VMEM] * 4,
        moved=2 << 20,
    )
    one, two, three = shift_second(one, -1), shift_second(two, -2), shift_second(three, -3)
    attended = call(
        finish_kernel,
        shape((count, queries.shape[2]), bf16),
        (own, one, two, three, queries.reshape(count, queries.shape[2]), peak, mass, past),
        [VMEM] * 8,
        VMEM,
        moved=1 << 20,
    )
    return new_master, new_first, new_second, attended.reshape(queries.shape)


def solution(mesh):
    in_specs = (
        P(("fsdp", "rep"), "tp"),
        P(("fsdp", "rep"), "tp"),
        P(("fsdp", "rep"), "tp"),
        P(("fsdp", "rep"), "tp"),
        P(("fsdp", "rep"), "tp"),
        P(None, ("fsdp", "rep"), None),
        P(None, ("fsdp", "rep"), "tp"),
        P(("fsdp", "rep"), None, "tp"),
        P(("fsdp", "rep")),
    )
    out_specs = (
        P(("fsdp", "rep"), "tp"),
        P(("fsdp", "rep"), "tp"),
        P(("fsdp", "rep"), "tp"),
        P(None, ("fsdp", "rep"), "tp"),
    )
    return jax.shard_map(body, mesh=mesh, in_specs=in_specs, out_specs=out_specs, check_vma=False)
```

```python
import functools
import math

import jax
import jax.numpy as jnp
from jax import lax
from jax.experimental import pallas as pl
from jax.experimental.pallas import tpu as pltpu
from jax.sharding import PartitionSpec as P

HEADS = 64
KVH = 8
HD = 128
ADAM_STEP = 100

learn_rate = 0.001
beta_one = 0.9
beta_two = 0.95
decay_rate = 0.1
tiny_term = 1e-08

NY, NX, NZ = 4, 4, 8
AXES = ("fsdp", "tp", "rep")
VMEM_LIMIT = 40 * 1024 * 1024
f32 = jnp.float32
bf16 = jnp.bfloat16


def pairs_of(move):
    pairs = []
    for y in range(NY):
        for k in range(2):
            for x in range(NX):
                for z in range(NZ):
                    v, j, u, w = move(y, k, x, z)
                    source = ((y * 2 + k) * NZ + z) * NX + x
                    target = (((v % NY) * 2 + j) * NZ + w % NZ) * NX + u % NX
                    pairs.append((source, target))
    return pairs


def swap_core(a):
    return lax.ppermute(a, AXES, pairs_of(lambda y, k, x, z: (y, 1 - k, x, z)))


def pass_on(a):
    return lax.ppermute(a, AXES, pairs_of(lambda y, k, x, z: (y, k, x, z + 1 - 2 * k)))


def pass_last(a):
    pairs = pairs_of(lambda y, k, x, z: (y, k, x, z - 1))
    return lax.ppermute(a, AXES, [m for m in pairs if m[0] // (NX * NZ) % 2 == 1])


def shift_first(a, d):
    return lax.ppermute(
        a, AXES, pairs_of(lambda y, k, x, z: (y, k, x + d, z) if k == 0 else (y + d, k, x, z))
    )


def shift_second(a, d):
    return lax.ppermute(
        a, AXES, pairs_of(lambda y, k, x, z: (y + d, k, x, z) if k == 0 else (y, k, x + d, z))
    )


def to_owner(a):
    return lax.ppermute(
        a, AXES, pairs_of(lambda y, k, x, z: (z // 2, z % 2, x, z + 4 * k - y))
    )


SMEM = pl.BlockSpec(memory_space=pltpu.SMEM)
VMEM = pl.BlockSpec(memory_space=pltpu.VMEM)
ANY = pl.BlockSpec(memory_space=pl.ANY)


def call(kernel, out, args, in_specs, out_specs, scratch=(), aliases=None, flops=0, moved=0):
    return pl.pallas_call(
        kernel,
        out_shape=out,
        in_specs=in_specs,
        out_specs=out_specs,
        scratch_shapes=list(scratch),
        input_output_aliases=aliases or {},
        cost_estimate=pl.CostEstimate(flops=flops, bytes_accessed=moved, transcendentals=0),
        compiler_params=pltpu.CompilerParams(vmem_limit_bytes=VMEM_LIMIT),
    )(*args)


def shape(dims, dtype):
    return jax.ShapeDtypeStruct(dims, dtype)


def after_all(value, *others):
    def kernel(*refs):
        pass

    return call(
        kernel,
        shape(value.shape, value.dtype),
        (value, *others),
        [ANY] * (1 + len(others)),
        ANY,
        aliases={0: 0},
    )


def partial_kernel(step, *refs):
    place, own_x, other_x, block, other_block = refs[:5]
    keep, one, two, three, token, turned = refs[-6:]
    k, p = place[0], place[1]
    slot = jnp.where(k == 0, step, 4 - step)
    token[...] = jnp.zeros_like(token)

    def turn():
        turned[0] = block[...].T
        turned[1] = other_block[...].T

    def tile(a):
        at = pl.ds(pl.multiple_of(a * 256, 256), 256)
        return jnp.dot(turned[0], own_x[:, at], preferred_element_type=f32) + jnp.dot(
            turned[1], other_x[:, at], preferred_element_type=f32
        )

    if step == 4:

        @pl.when(k == 1)
        def _():
            turn()
            for d, out in enumerate((keep, one, two, three)):

                @pl.when(lax.rem(p + d, 4) == 0)
                def _():
                    for a in range(4):
                        out[a] = tile(a).astype(out.dtype)

        return

    @pl.when(slot < 4)
    def _():
        turn()

        def one_tile(i, carry):
            a = jnp.where(k == 0, lax.rem(p + i, 4), i)
            d = jnp.where(k == 0, i, lax.rem(slot - p + 4, 4))
            index = jnp.where(k == 0, slot, i)
            result = tile(a)

            @pl.when(d == 0)
            def _():
                keep[index] = result

            for m, out in ((1, one), (2, two), (3, three)):

                @pl.when(d == m)
                def _():
                    out[index] = result.astype(bf16)

            return carry

        lax.fori_loop(0, 4, one_tile, 0)


def middle_kernel(place, keep, one, two, three, *refs):
    own, s_one, s_two, s_three = refs[3:]
    q = place[2]
    for d, out in enumerate((own, s_one, s_two, s_three)):
        j = lax.rem(q + d, 4)
        out[...] = (
            keep[j] + one[j].astype(f32) + two[j].astype(f32) + three[j].astype(f32)
        ).astype(out.dtype)


def adam_kernel(gradient, master, first_moment, second_moment, *outs):
    new_master, new_first, new_second, weight = outs
    gradient = gradient[...].astype(f32).T
    first = beta_one * first_moment[...].astype(f32) + (1.0 - beta_one) * gradient
    second = beta_two * second_moment[...].astype(f32) + (1.0 - beta_two) * gradient * gradient
    corr_one = 1.0 - beta_one**ADAM_STEP
    corr_two = 1.0 - beta_two**ADAM_STEP
    update = first / corr_one / (jnp.sqrt(second / corr_two) + tiny_term)
    update = update + decay_rate * master[...]
    result = master[...] - learn_rate * update
    new_master[...] = result
    new_first[...] = first.astype(bf16)
    new_second[...] = second.astype(bf16)
    weight[...] = result.astype(bf16)


def states_kernel(place, states, *refs):
    sends, token, sems = refs[:4], refs[4], refs[5]
    k, p, q = place[0], place[1], place[2]
    copies = []
    for m in range(4):
        for n in range(4):
            u, v = lax.rem(p + m, 4), lax.rem(q + n, 4)
            x = jnp.where(k == 0, u, v)
            y = jnp.where(k == 0, v, u)
            for i, core in enumerate((k, 1 - k)):
                at = pl.multiple_of(((2 * y + core) * 4 + x) * 256, 256)
                copies.append(
                    pltpu.make_async_copy(
                        states.at[:, pl.ds(at, 256)], sends[m].at[n, i], sems.at[len(copies)]
                    )
                )
                copies[-1].start()
    token[...] = jnp.zeros_like(token)
    for copy in copies:
        copy.wait()


def regroup_kernel(*refs):
    came, sends, token = refs[:4], refs[4:8], refs[8]
    token[...] = jnp.zeros_like(token)
    for n in range(4):
        for m in range(4):
            sends[n][m] = came[m][n]


def project_kernel(weight, other_weight, *refs):
    states, sends = refs[:4], refs[4:]
    for m, out in enumerate(sends):
        for n in range(4):
            term = jnp.dot(states[n][m, 0], weight[...], preferred_element_type=f32)
            term = term + jnp.dot(states[n][m, 1], other_weight[...], preferred_element_type=f32)
            out[n] = term.astype(out.dtype)


def gather_kernel(keep, one, two, three, *outs):
    for n, out in enumerate(outs):
        out[...] = (
            keep[n] + one[n].astype(f32) + two[n].astype(f32) + three[n].astype(f32)
        ).astype(out.dtype)


def finish_kernel(own, one, two, three, queries, peak, mass, past, out):
    fresh = own[...] + one[...].astype(f32) + two[...].astype(f32) + three[...].astype(f32)
    fresh = fresh.astype(bf16)
    n = fresh.shape[0]
    rows = n // 4
    group = HEADS // KVH
    line = lax.broadcasted_iota(jnp.int32, (n, n), 0)
    lane = lax.broadcasted_iota(jnp.int32, (n, n), 1)
    seen = (lax.rem(line, rows) == lax.rem(lane, rows)) & (lane <= line)
    seen = jnp.concatenate([seen.astype(f32)] * group, axis=0) > 0.5
    scale = 1.0 / math.sqrt(HD)
    keys, values = fresh[:, :HD], fresh[:, HD:]
    stack = jnp.concatenate([queries[:, g * HD : g * HD + HD] for g in range(group)], axis=0)
    scores = lax.dot_general(
        stack, keys, (((1,), (1,)), ((), ())), preferred_element_type=f32
    )
    scores = jnp.where(seen, scores * scale, -1e30)
    before = jnp.concatenate([peak[:, g : g + 1] for g in range(group)], axis=0)
    mass = jnp.concatenate([mass[:, g : g + 1] for g in range(group)], axis=0)
    top = jnp.maximum(before, jnp.max(scores, axis=1, keepdims=True))
    weight = jnp.where(seen, jnp.exp(scores - top), 0.0)
    fade = jnp.exp(before - top)
    total = mass * fade + jnp.sum(weight, axis=1, keepdims=True)
    share = 1.0 / total
    probs = (weight * share).astype(bf16)
    result = jnp.dot(probs, values, preferred_element_type=f32)
    result = (result + past[...] * (fade * share)).astype(bf16)
    for g in range(group):
        out[:, g * HD : g * HD + HD] = result[g * n : g * n + n]


def past_part(queries, cache, lengths):
    steps, rows = queries.shape[0], queries.shape[1]
    span = cache.shape[1]
    group = HEADS // KVH
    block = queries.reshape(steps, rows, group, HD)
    scores = jnp.einsum(
        "srgd,rtd->srgt", block, cache[:, :, :HD], preferred_element_type=f32
    ) * (1.0 / math.sqrt(HD))
    live = jnp.arange(span, dtype=jnp.int32)[None, :] < lengths[:, None]
    scores = jnp.where(live[None, :, None, :], scores, -jnp.inf)
    peak = jnp.max(scores, axis=-1)
    weight = jnp.exp(scores - peak[..., None])
    mass = jnp.sum(weight, axis=-1)
    past = jnp.einsum(
        "srgt,rtd->gsrd", weight.astype(bf16), cache[:, :, HD:], preferred_element_type=f32
    )
    n = steps * rows
    return peak.reshape(n, group), mass.reshape(n, group), past.reshape(n * group, HD)


def body(
    train_inputs,
    kv_grads,
    master,
    first_moment,
    second_moment,
    hidden_states,
    queries,
    kv_cache,
    cache_lengths,
):
    f = lax.axis_index("fsdp")
    x = lax.axis_index("rep")
    y, k = f // 2, f % 2
    p = jnp.where(k == 0, x, y)
    q = jnp.where(k == 0, y, x)
    place = jnp.stack([k, p, q]).astype(jnp.int32)
    steps, rows, width = hidden_states.shape
    count = steps * rows

    block = kv_grads
    other_block = swap_core(kv_grads)
    other_x = swap_core(train_inputs)

    part = (4, 256, 256)
    buffers = ()
    outs = (shape(part, f32),) + (shape(part, bf16),) * 3 + (shape((8, 128), f32),)

    def add_slot(step, block, other_block, buffers, awaited=()):
        first = not buffers
        *buffers, token = call(
            functools.partial(partial_kernel, step),
            outs,
            (place, train_inputs, other_x, block, other_block, *buffers, *awaited),
            [SMEM] + [VMEM] * (4 + len(buffers)) + [ANY] * len(awaited),
            [VMEM] * 5,
            [pltpu.VMEM((2, 256, 640), bf16)],
            {} if first else {5: 0, 6: 1, 7: 2, 8: 3},
            flops=4 * 640 * 1024 * 256,
            moved=6 << 20,
        )
        return tuple(buffers), token

    group = (4, 2, count, 256)
    *sends, packed = call(
        states_kernel,
        (shape(group, bf16),) * 4 + (shape((8, 128), f32),),
        (place, hidden_states.reshape(count, width)),
        [SMEM, pl.BlockSpec(memory_space=pltpu.HBM)],
        [VMEM] * 5,
        [pltpu.SemaphoreType.DMA((32,))],
        moved=4 << 20,
    )
    other_block = after_all(other_block, packed)
    came = [sends[0]] + [shift_first(sends[d], d) for d in (1, 2, 3)]
    *sends, regrouped = call(
        regroup_kernel,
        (shape(group, bf16),) * 4 + (shape((8, 128), f32),),
        tuple(came),
        [VMEM] * 4,
        [VMEM] * 5,
        moved=4 << 20,
    )
    states = [sends[0]] + [shift_second(sends[d], d) for d in (1, 2, 3)]

    tokens = []
    arrived = (block, other_block)
    for step in range(5):
        if 0 < step < 4:
            awaited = (tokens[-1], regrouped) if step == 3 else (tokens[-1],)
            arrived = (arrived[0], after_all(arrived[1], *awaited))
        if step < 4:
            send = pass_on if step < 3 else pass_last
            after = (send(arrived[0]), send(arrived[1]))
        buffers, token = add_slot(step, *arrived, buffers)
        tokens.append(token)
        arrived = after

    keep, one, two, three = buffers
    peak, mass, past = past_part(queries, kv_cache, cache_lengths)
    three = after_all(three, *states[1:])
    one, two, three = shift_first(one, 1), shift_first(two, 2), shift_first(three, 3)
    square, narrow = shape((256, 256), f32), shape((256, 256), bf16)
    own, one, two, three = call(
        middle_kernel,
        (square, narrow, narrow, narrow),
        (place, keep, one, two, three, past, peak, mass),
        [SMEM] + [VMEM] * 4 + [ANY] * 3,
        [VMEM] * 4,
        moved=4 << 20,
    )
    one, two, three = shift_second(one, 1), shift_second(two, 2), shift_second(three, 3)
    gradient = own + one.astype(f32) + two.astype(f32) + three.astype(f32)
    gradient = gradient.astype(bf16)
    gradient = to_owner(gradient)
    new_master, new_first, new_second, weight = call(
        adam_kernel,
        (square, narrow, narrow, narrow),
        (gradient, master, first_moment, second_moment),
        [VMEM] * 4,
        [VMEM] * 4,
        moved=1 << 20,
    )

    part = (4, count, 256)
    keep, one, two, three = call(
        project_kernel,
        (shape(part, f32),) + (shape(part, bf16),) * 3,
        (weight, swap_core(weight), *states),
        [VMEM] * 6,
        [VMEM] * 4,
        flops=2 * 16 * count * 512 * 256,
        moved=4 << 20,
    )
    one, two, three = shift_first(one, -1), shift_first(two, -2), shift_first(three, -3)
    result, sent = shape((count, 256), f32), shape((count, 256), bf16)
    own, one, two, three = call(
        gather_kernel,
        (result, sent, sent, sent),
        (keep, one, two, three),
        [VMEM] * 4,
        [VMEM] * 4,
        moved=2 << 20,
    )
    one, two, three = shift_second(one, -1), shift_second(two, -2), shift_second(three, -3)
    attended = call(
        finish_kernel,
        shape((count, queries.shape[2]), bf16),
        (own, one, two, three, queries.reshape(count, queries.shape[2]), peak, mass, past),
        [VMEM] * 8,
        VMEM,
        moved=1 << 20,
    )
    return new_master, new_first, new_second, attended.reshape(queries.shape)


def solution(mesh):
    in_specs = (
        P(("fsdp", "rep"), "tp"),
        P(("fsdp", "rep"), "tp"),
        P(("fsdp", "rep"), "tp"),
        P(("fsdp", "rep"), "tp"),
        P(("fsdp", "rep"), "tp"),
        P(None, ("fsdp", "rep"), None),
        P(None, ("fsdp", "rep"), "tp"),
        P(("fsdp", "rep"), None, "tp"),
        P(("fsdp", "rep")),
    )
    out_specs = (
        P(("fsdp", "rep"), "tp"),
        P(("fsdp", "rep"), "tp"),
        P(("fsdp", "rep"), "tp"),
        P(None, ("fsdp", "rep"), "tp"),
    )
    return jax.shard_map(body, mesh=mesh, in_specs=in_specs, out_specs=out_specs, check_vma=False)
```

```python
import functools
import math

import jax
import jax.numpy as jnp
from jax import lax
from jax.experimental import pallas as pl
from jax.experimental.pallas import tpu as pltpu
from jax.sharding import PartitionSpec as P

HEADS = 64
KVH = 8
HD = 128
ADAM_STEP = 100

learn_rate = 0.001
beta_one = 0.9
beta_two = 0.95
decay_rate = 0.1
tiny_term = 1e-08

NY, NX, NZ = 4, 4, 8
AXES = ("fsdp", "tp", "rep")
VMEM_LIMIT = 40 * 1024 * 1024
f32 = jnp.float32
bf16 = jnp.bfloat16


def pairs_of(move):
    pairs = []
    for y in range(NY):
        for k in range(2):
            for x in range(NX):
                for z in range(NZ):
                    v, j, u, w = move(y, k, x, z)
                    source = ((y * 2 + k) * NZ + z) * NX + x
                    target = (((v % NY) * 2 + j) * NZ + w % NZ) * NX + u % NX
                    pairs.append((source, target))
    return pairs


def swap_core(a):
    return lax.ppermute(a, AXES, pairs_of(lambda y, k, x, z: (y, 1 - k, x, z)))


def pass_on(a):
    return lax.ppermute(a, AXES, pairs_of(lambda y, k, x, z: (y, k, x, z + 1 - 2 * k)))


def pass_last(a):
    pairs = pairs_of(lambda y, k, x, z: (y, k, x, z - 1))
    return lax.ppermute(a, AXES, [m for m in pairs if m[0] // (NX * NZ) % 2 == 1])


def shift_first(a, d):
    return lax.ppermute(
        a, AXES, pairs_of(lambda y, k, x, z: (y, k, x + d, z) if k == 0 else (y + d, k, x, z))
    )


def shift_second(a, d):
    return lax.ppermute(
        a, AXES, pairs_of(lambda y, k, x, z: (y + d, k, x, z) if k == 0 else (y, k, x + d, z))
    )


def to_owner(a):
    return lax.ppermute(
        a, AXES, pairs_of(lambda y, k, x, z: (z // 2, z % 2, x, z + 4 * k - y))
    )


SMEM = pl.BlockSpec(memory_space=pltpu.SMEM)
VMEM = pl.BlockSpec(memory_space=pltpu.VMEM)
ANY = pl.BlockSpec(memory_space=pl.ANY)


def call(kernel, out, args, in_specs, out_specs, scratch=(), aliases=None, flops=0, moved=0):
    return pl.pallas_call(
        kernel,
        out_shape=out,
        in_specs=in_specs,
        out_specs=out_specs,
        scratch_shapes=list(scratch),
        input_output_aliases=aliases or {},
        cost_estimate=pl.CostEstimate(flops=flops, bytes_accessed=moved, transcendentals=0),
        compiler_params=pltpu.CompilerParams(vmem_limit_bytes=VMEM_LIMIT),
    )(*args)


def shape(dims, dtype):
    return jax.ShapeDtypeStruct(dims, dtype)


def after_all(value, *others):
    def kernel(*refs):
        pass

    return call(
        kernel,
        shape(value.shape, value.dtype),
        (value, *others),
        [ANY] * (1 + len(others)),
        ANY,
        aliases={0: 0},
    )


def partial_kernel(step, *refs):
    place, own_x, other_x, block, other_block = refs[:5]
    keep, one, two, three, token, turned = refs[-6:]
    k, p = place[0], place[1]
    token[...] = jnp.zeros_like(token)

    def turn():
        turned[0] = block[...].T
        turned[1] = other_block[...].T

    def tile(a):
        at = pl.ds(pl.multiple_of(a * 256, 256), 256)
        return jnp.dot(turned[0], own_x[:, at], preferred_element_type=f32) + jnp.dot(
            turned[1], other_x[:, at], preferred_element_type=f32
        )

    if step == 4:

        @pl.when(k == 1)
        def _():
            turn()
            for d, out in enumerate((keep, one, two, three)):

                @pl.when(lax.rem(p + d, 4) == 0)
                def _():
                    for a in range(4):
                        out[a] = tile(a).astype(out.dtype)

        return

    @pl.when(k == 0)
    def _():
        turn()
        for d, out in enumerate((keep, one, two, three)):
            out[step] = tile(lax.rem(p + d, 4)).astype(out.dtype)

    if step > 0:

        @pl.when(k == 1)
        def _():
            turn()
            for d, out in enumerate((keep, one, two, three)):

                @pl.when(lax.rem(p + d, 4) == 4 - step)
                def _():
                    def one_tile(a, carry):
                        out[a] = tile(a).astype(out.dtype)
                        return carry

                    lax.fori_loop(0, 4, one_tile, 0)


def middle_kernel(place, keep, one, two, three, *refs):
    own, s_one, s_two, s_three = refs[3:]
    q = place[2]
    for d, out in enumerate((own, s_one, s_two, s_three)):
        j = lax.rem(q + d, 4)
        out[...] = (
            keep[j] + one[j].astype(f32) + two[j].astype(f32) + three[j].astype(f32)
        ).astype(out.dtype)


def adam_kernel(gradient, master, first_moment, second_moment, *outs):
    new_master, new_first, new_second, weight = outs
    gradient = gradient[...].astype(f32).T
    first = beta_one * first_moment[...].astype(f32) + (1.0 - beta_one) * gradient
    second = beta_two * second_moment[...].astype(f32) + (1.0 - beta_two) * gradient * gradient
    corr_one = 1.0 - beta_one**ADAM_STEP
    corr_two = 1.0 - beta_two**ADAM_STEP
    update = first / corr_one / (jnp.sqrt(second / corr_two) + tiny_term)
    update = update + decay_rate * master[...]
    result = master[...] - learn_rate * update
    new_master[...] = result
    new_first[...] = first.astype(bf16)
    new_second[...] = second.astype(bf16)
    weight[...] = result.astype(bf16)


def states_kernel(place, states, *refs):
    sends, token, sems = refs[:4], refs[4], refs[5]
    k, p, q = place[0], place[1], place[2]
    copies = []
    for m in range(4):
        for n in range(4):
            u, v = lax.rem(p + m, 4), lax.rem(q + n, 4)
            x = jnp.where(k == 0, u, v)
            y = jnp.where(k == 0, v, u)
            for i, core in enumerate((k, 1 - k)):
                at = pl.multiple_of(((2 * y + core) * 4 + x) * 256, 256)
                copies.append(
                    pltpu.make_async_copy(
                        states.at[:, pl.ds(at, 256)], sends[n].at[m, i], sems.at[len(copies)]
                    )
                )
                copies[-1].start()
    token[...] = jnp.zeros_like(token)
    for copy in copies:
        copy.wait()


def project_kernel(*refs):
    weights, states, outs = refs[:4], refs[4:8], refs[8:]
    for n, out in enumerate(outs):
        total = None
        for m in range(4):
            for i in range(2):
                term = jnp.dot(states[n][m, i], weights[m][i], preferred_element_type=f32)
                total = term if total is None else total + term
        out[...] = total.astype(out.dtype)


def finish_kernel(own, one, two, three, queries, peak, mass, past, out):
    fresh = own[...] + one[...].astype(f32) + two[...].astype(f32) + three[...].astype(f32)
    fresh = fresh.astype(bf16)
    n = fresh.shape[0]
    rows = n // 4
    group = HEADS // KVH
    line = lax.broadcasted_iota(jnp.int32, (n, n), 0)
    lane = lax.broadcasted_iota(jnp.int32, (n, n), 1)
    seen = (lax.rem(line, rows) == lax.rem(lane, rows)) & (lane <= line)
    unseen = jnp.where(seen, 0.0, -1e30)
    scale = 1.0 / math.sqrt(HD)
    keys, values = fresh[:, :HD], fresh[:, HD:]
    stack = jnp.concatenate([queries[:, g * HD : g * HD + HD] for g in range(group)], axis=0)
    scores = lax.dot_general(
        stack, keys, (((1,), (1,)), ((), ())), preferred_element_type=f32
    )
    scores = scores.reshape(group, n, n) * scale + unseen[None]
    before = jnp.stack([peak[:, g : g + 1] for g in range(group)])
    mass = jnp.stack([mass[:, g : g + 1] for g in range(group)])
    top = jnp.maximum(before, jnp.max(scores, axis=2, keepdims=True))
    weight = jnp.exp(scores - top)
    fade = jnp.exp(before - top)
    share = 1.0 / (mass * fade + jnp.sum(weight, axis=2, keepdims=True))
    probs = (weight * share).astype(bf16).reshape(group * n, n)
    result = jnp.dot(probs, values, preferred_element_type=f32)
    old = past[...].reshape(group, n, HD) * (fade * share)
    result = (result + old.reshape(group * n, HD)).astype(bf16)
    for g in range(group):
        out[:, g * HD : g * HD + HD] = result[g * n : g * n + n]


def past_part(queries, cache, lengths):
    steps, rows = queries.shape[0], queries.shape[1]
    span = cache.shape[1]
    group = HEADS // KVH
    block = queries.reshape(steps, rows, group, HD)
    scores = jnp.einsum(
        "srgd,rtd->srgt", block, cache[:, :, :HD], preferred_element_type=f32
    ) * (1.0 / math.sqrt(HD))
    live = jnp.arange(span, dtype=jnp.int32)[None, :] < lengths[:, None]
    scores = jnp.where(live[None, :, None, :], scores, -jnp.inf)
    peak = jnp.max(scores, axis=-1)
    weight = jnp.exp(scores - peak[..., None])
    mass = jnp.sum(weight, axis=-1)
    past = jnp.einsum(
        "srgt,rtd->gsrd", weight.astype(bf16), cache[:, :, HD:], preferred_element_type=f32
    )
    n = steps * rows
    return peak.reshape(n, group), mass.reshape(n, group), past.reshape(n * group, HD)


def body(
    train_inputs,
    kv_grads,
    master,
    first_moment,
    second_moment,
    hidden_states,
    queries,
    kv_cache,
    cache_lengths,
):
    f = lax.axis_index("fsdp")
    x = lax.axis_index("rep")
    y, k = f // 2, f % 2
    p = jnp.where(k == 0, x, y)
    q = jnp.where(k == 0, y, x)
    place = jnp.stack([k, p, q]).astype(jnp.int32)
    steps, rows, width = hidden_states.shape
    count = steps * rows

    block = kv_grads
    other_block = swap_core(kv_grads)
    other_x = swap_core(train_inputs)

    part = (4, 256, 256)
    buffers = ()
    outs = (shape(part, f32),) + (shape(part, bf16),) * 3 + (shape((8, 128), f32),)

    def add_slot(step, block, other_block, buffers, awaited=()):
        first = not buffers
        *buffers, token = call(
            functools.partial(partial_kernel, step),
            outs,
            (place, train_inputs, other_x, block, other_block, *buffers, *awaited),
            [SMEM] + [VMEM] * (4 + len(buffers)) + [ANY] * len(awaited),
            [VMEM] * 5,
            [pltpu.VMEM((2, 256, 640), bf16)],
            {} if first else {5: 0, 6: 1, 7: 2, 8: 3},
            flops=4 * 640 * 1024 * 256,
            moved=6 << 20,
        )
        return tuple(buffers), token

    group = (4, 2, count, 256)
    *sends, packed = call(
        states_kernel,
        (shape(group, bf16),) * 4 + (shape((8, 128), f32),),
        (place, hidden_states.reshape(count, width)),
        [SMEM, pl.BlockSpec(memory_space=pltpu.HBM)],
        [VMEM] * 5,
        [pltpu.SemaphoreType.DMA((32,))],
        moved=4 << 20,
    )
    other_block = after_all(other_block, packed)
    states = [sends[0]] + [shift_second(sends[d], d) for d in (1, 2, 3)]

    tokens = []
    arrived = (block, other_block)
    for step in range(5):
        if 0 < step < 4:
            awaited = (tokens[-1], *states[1:]) if step == 3 else (tokens[-1],)
            arrived = (arrived[0], after_all(arrived[1], *awaited))
        if step < 4:
            send = pass_on if step < 3 else pass_last
            after = (send(arrived[0]), send(arrived[1]))
        buffers, token = add_slot(step, *arrived, buffers)
        tokens.append(token)
        arrived = after

    keep, one, two, three = buffers
    peak, mass, past = past_part(queries, kv_cache, cache_lengths)
    one, two, three = shift_first(one, 1), shift_first(two, 2), shift_first(three, 3)
    square, narrow = shape((256, 256), f32), shape((256, 256), bf16)
    own, one, two, three = call(
        middle_kernel,
        (square, narrow, narrow, narrow),
        (place, keep, one, two, three, past, peak, mass),
        [SMEM] + [VMEM] * 4 + [ANY] * 3,
        [VMEM] * 4,
        moved=4 << 20,
    )
    one, two, three = shift_second(one, 1), shift_second(two, 2), shift_second(three, 3)
    gradient = own + one.astype(f32) + two.astype(f32) + three.astype(f32)
    gradient = gradient.astype(bf16)
    gradient = to_owner(gradient)
    new_master, new_first, new_second, weight = call(
        adam_kernel,
        (square, narrow, narrow, narrow),
        (gradient, master, first_moment, second_moment),
        [VMEM] * 4,
        [VMEM] * 4,
        moved=1 << 20,
    )

    pair = jnp.stack([weight, swap_core(weight)])
    line = [pair, shift_first(pair, -1), shift_first(pair, 2), shift_first(pair, 1)]
    result, sent = shape((count, 256), f32), shape((count, 256), bf16)
    own, one, two, three = call(
        project_kernel,
        (result, sent, sent, sent),
        (*line, *states),
        [VMEM] * 8,
        [VMEM] * 4,
        flops=2 * 16 * count * 512 * 256,
        moved=4 << 20,
    )
    one, two, three = shift_second(one, -1), shift_second(two, -2), shift_second(three, -3)
    attended = call(
        finish_kernel,
        shape((count, queries.shape[2]), bf16),
        (own, one, two, three, queries.reshape(count, queries.shape[2]), peak, mass, past),
        [VMEM] * 8,
        VMEM,
        moved=1 << 20,
    )
    return new_master, new_first, new_second, attended.reshape(queries.shape)


def solution(mesh):
    in_specs = (
        P(("fsdp", "rep"), "tp"),
        P(("fsdp", "rep"), "tp"),
        P(("fsdp", "rep"), "tp"),
        P(("fsdp", "rep"), "tp"),
        P(("fsdp", "rep"), "tp"),
        P(None, ("fsdp", "rep"), None),
        P(None, ("fsdp", "rep"), "tp"),
        P(("fsdp", "rep"), None, "tp"),
        P(("fsdp", "rep")),
    )
    out_specs = (
        P(("fsdp", "rep"), "tp"),
        P(("fsdp", "rep"), "tp"),
        P(("fsdp", "rep"), "tp"),
        P(None, ("fsdp", "rep"), "tp"),
    )
    return jax.shard_map(body, mesh=mesh, in_specs=in_specs, out_specs=out_specs, check_vma=False)
```

```python
import functools
import math

import jax
import jax.numpy as jnp
from jax import lax
from jax.experimental import pallas as pl
from jax.experimental.pallas import tpu as pltpu
from jax.sharding import PartitionSpec as P

HEADS = 64
KVH = 8
HD = 128
ADAM_STEP = 100

learn_rate = 0.001
beta_one = 0.9
beta_two = 0.95
decay_rate = 0.1
tiny_term = 1e-08

NY, NX, NZ = 4, 4, 8
AXES = ("fsdp", "tp", "rep")
VMEM_LIMIT = 40 * 1024 * 1024
f32 = jnp.float32
bf16 = jnp.bfloat16


def pairs_of(move):
    pairs = []
    for y in range(NY):
        for k in range(2):
            for x in range(NX):
                for z in range(NZ):
                    v, j, u, w = move(y, k, x, z)
                    source = ((y * 2 + k) * NZ + z) * NX + x
                    target = (((v % NY) * 2 + j) * NZ + w % NZ) * NX + u % NX
                    pairs.append((source, target))
    return pairs


def swap_core(a):
    return lax.ppermute(a, AXES, pairs_of(lambda y, k, x, z: (y, 1 - k, x, z)))


def pass_on(a):
    return lax.ppermute(a, AXES, pairs_of(lambda y, k, x, z: (y, k, x, z + 1 - 2 * k)))


def pass_last(a):
    pairs = pairs_of(lambda y, k, x, z: (y, k, x, z - 1))
    return lax.ppermute(a, AXES, [m for m in pairs if m[0] // (NX * NZ) % 2 == 1])


def shift_first(a, d):
    return lax.ppermute(
        a, AXES, pairs_of(lambda y, k, x, z: (y, k, x + d, z) if k == 0 else (y + d, k, x, z))
    )


def shift_second(a, d):
    return lax.ppermute(
        a, AXES, pairs_of(lambda y, k, x, z: (y + d, k, x, z) if k == 0 else (y, k, x + d, z))
    )


def to_owner(a):
    return lax.ppermute(
        a, AXES, pairs_of(lambda y, k, x, z: (z // 2, z % 2, x, z + 4 * k - y))
    )


SMEM = pl.BlockSpec(memory_space=pltpu.SMEM)
VMEM = pl.BlockSpec(memory_space=pltpu.VMEM)
ANY = pl.BlockSpec(memory_space=pl.ANY)


def call(kernel, out, args, in_specs, out_specs, scratch=(), aliases=None, flops=0, moved=0):
    return pl.pallas_call(
        kernel,
        out_shape=out,
        in_specs=in_specs,
        out_specs=out_specs,
        scratch_shapes=list(scratch),
        input_output_aliases=aliases or {},
        cost_estimate=pl.CostEstimate(flops=flops, bytes_accessed=moved, transcendentals=0),
        compiler_params=pltpu.CompilerParams(vmem_limit_bytes=VMEM_LIMIT),
    )(*args)


def shape(dims, dtype):
    return jax.ShapeDtypeStruct(dims, dtype)


def after_all(value, *others):
    def kernel(*refs):
        pass

    return call(
        kernel,
        shape(value.shape, value.dtype),
        (value, *others),
        [ANY] * (1 + len(others)),
        ANY,
        aliases={0: 0},
    )


def partial_kernel(step, *refs):
    place, own_x, other_x, block, other_block = refs[:5]
    keep, one, two, three, token, turned = refs[-6:]
    k, p = place[0], place[1]
    token[...] = jnp.zeros_like(token)

    def turn():
        turned[0] = block[...].T
        turned[1] = other_block[...].T

    def tile(a):
        at = pl.ds(pl.multiple_of(a * 256, 256), 256)
        return jnp.dot(turned[0], own_x[:, at], preferred_element_type=f32) + jnp.dot(
            turned[1], other_x[:, at], preferred_element_type=f32
        )

    if step == 4:

        @pl.when(k == 1)
        def _():
            turn()
            for d, out in enumerate((keep, one, two, three)):

                @pl.when(lax.rem(p + d, 4) == 0)
                def _():
                    for a in range(4):
                        out[a] = tile(a).astype(out.dtype)

        return

    @pl.when(k == 0)
    def _():
        turn()
        for d, out in enumerate((keep, one, two, three)):
            out[step] = tile(lax.rem(p + d, 4)).astype(out.dtype)

    if step > 0:

        @pl.when(k == 1)
        def _():
            turn()
            for d, out in enumerate((keep, one, two, three)):

                @pl.when(lax.rem(p + d, 4) == 4 - step)
                def _():
                    def one_tile(a, carry):
                        out[a] = tile(a).astype(out.dtype)
                        return carry

                    lax.fori_loop(0, 4, one_tile, 0)


def middle_kernel(place, keep, one, two, three, *refs):
    own, s_one, s_two, s_three = refs[3:]
    q = place[2]
    for d, out in enumerate((own, s_one, s_two, s_three)):
        j = lax.rem(q + d, 4)
        out[...] = (
            keep[j] + one[j].astype(f32) + two[j].astype(f32) + three[j].astype(f32)
        ).astype(out.dtype)


def adam_kernel(gradient, master, first_moment, second_moment, *outs):
    new_master, new_first, new_second, weight = outs
    gradient = gradient[...].astype(f32).T
    first = beta_one * first_moment[...].astype(f32) + (1.0 - beta_one) * gradient
    second = beta_two * second_moment[...].astype(f32) + (1.0 - beta_two) * gradient * gradient
    corr_one = 1.0 - beta_one**ADAM_STEP
    corr_two = 1.0 - beta_two**ADAM_STEP
    update = first / corr_one / (jnp.sqrt(second / corr_two) + tiny_term)
    update = update + decay_rate * master[...]
    result = master[...] - learn_rate * update
    new_master[...] = result
    new_first[...] = first.astype(bf16)
    new_second[...] = second.astype(bf16)
    weight[...] = result.astype(bf16)


def states_kernel(place, states, *refs):
    sends, token, sems = refs[:4], refs[4], refs[5]
    k, p, q = place[0], place[1], place[2]
    copies = []
    for m in range(4):
        for n in range(4):
            u, v = lax.rem(p + m, 4), lax.rem(q + n, 4)
            x = jnp.where(k == 0, u, v)
            y = jnp.where(k == 0, v, u)
            for i, core in enumerate((k, 1 - k)):
                at = pl.multiple_of(((2 * y + core) * 4 + x) * 256, 256)
                copies.append(
                    pltpu.make_async_copy(
                        states.at[:, pl.ds(at, 256)], sends[n].at[m, i], sems.at[len(copies)]
                    )
                )
                copies[-1].start()
    token[...] = jnp.zeros_like(token)
    for copy in copies:
        copy.wait()


def project_kernel(*refs):
    weights, states, outs = refs[:4], refs[4:8], refs[8:]
    for n, out in enumerate(outs):
        total = None
        for m in range(4):
            for i in range(2):
                term = jnp.dot(states[n][m, i], weights[m][i], preferred_element_type=f32)
                total = term if total is None else total + term
        out[...] = total.astype(out.dtype)


def finish_kernel(own, one, two, three, queries, peak, mass, past, out):
    fresh = own[...] + one[...].astype(f32) + two[...].astype(f32) + three[...].astype(f32)
    fresh = fresh.astype(bf16)
    n = fresh.shape[0]
    rows = n // 4
    group = HEADS // KVH
    line = lax.broadcasted_iota(jnp.int32, (n, n), 0)
    lane = lax.broadcasted_iota(jnp.int32, (n, n), 1)
    seen = (lax.rem(line, rows) == lax.rem(lane, rows)) & (lane <= line)
    unseen = jnp.where(seen, 0.0, -1e30)
    scale = 1.0 / math.sqrt(HD)
    keys, values = fresh[:, :HD], fresh[:, HD:]
    stack = jnp.concatenate([queries[:, g * HD : g * HD + HD] for g in range(group)], axis=0)
    scores = lax.dot_general(
        stack, keys, (((1,), (1,)), ((), ())), preferred_element_type=f32
    )
    scores = scores.reshape(group, n, n) * scale + unseen[None]
    before = jnp.stack([peak[:, g : g + 1] for g in range(group)])
    mass = jnp.stack([mass[:, g : g + 1] for g in range(group)])
    top = jnp.maximum(before, jnp.max(scores, axis=2, keepdims=True))
    weight = jnp.exp(scores - top)
    fade = jnp.exp(before - top)
    share = 1.0 / (mass * fade + jnp.sum(weight, axis=2, keepdims=True))
    probs = (weight * share).astype(bf16).reshape(group * n, n)
    result = jnp.dot(probs, values, preferred_element_type=f32)
    old = past[...].reshape(group, n, HD) * (fade * share)
    result = (result + old.reshape(group * n, HD)).astype(bf16)
    for g in range(group):
        out[:, g * HD : g * HD + HD] = result[g * n : g * n + n]


def past_part(queries, cache, lengths):
    steps, rows = queries.shape[0], queries.shape[1]
    span = cache.shape[1]
    group = HEADS // KVH
    block = queries.reshape(steps, rows, group, HD)
    scores = jnp.einsum(
        "srgd,rtd->srgt", block, cache[:, :, :HD], preferred_element_type=f32
    ) * (1.0 / math.sqrt(HD))
    live = jnp.arange(span, dtype=jnp.int32)[None, :] < lengths[:, None]
    scores = jnp.where(live[None, :, None, :], scores, -jnp.inf)
    peak = jnp.max(scores, axis=-1)
    weight = jnp.exp(scores - peak[..., None])
    mass = jnp.sum(weight, axis=-1)
    past = jnp.einsum(
        "srgt,rtd->gsrd", weight.astype(bf16), cache[:, :, HD:], preferred_element_type=f32
    )
    n = steps * rows
    return peak.reshape(n, group), mass.reshape(n, group), past.reshape(n * group, HD)


def body(
    train_inputs,
    kv_grads,
    master,
    first_moment,
    second_moment,
    hidden_states,
    queries,
    kv_cache,
    cache_lengths,
):
    f = lax.axis_index("fsdp")
    x = lax.axis_index("rep")
    y, k = f // 2, f % 2
    p = jnp.where(k == 0, x, y)
    q = jnp.where(k == 0, y, x)
    place = jnp.stack([k, p, q]).astype(jnp.int32)
    steps, rows, width = hidden_states.shape
    count = steps * rows

    block = kv_grads
    other_block = swap_core(kv_grads)
    other_x = swap_core(train_inputs)

    part = (4, 256, 256)
    buffers = ()
    outs = (shape(part, f32),) + (shape(part, bf16),) * 3 + (shape((8, 128), f32),)

    def add_slot(step, block, other_block, buffers, awaited=()):
        first = not buffers
        *buffers, token = call(
            functools.partial(partial_kernel, step),
            outs,
            (place, train_inputs, other_x, block, other_block, *buffers, *awaited),
            [SMEM] + [VMEM] * (4 + len(buffers)) + [ANY] * len(awaited),
            [VMEM] * 5,
            [pltpu.VMEM((2, 256, 640), bf16)],
            {} if first else {5: 0, 6: 1, 7: 2, 8: 3},
            flops=4 * 640 * 1024 * 256,
            moved=6 << 20,
        )
        return tuple(buffers), token

    group = (4, 2, count, 256)
    *sends, packed = call(
        states_kernel,
        (shape(group, bf16),) * 4 + (shape((8, 128), f32),),
        (place, hidden_states.reshape(count, width)),
        [SMEM, pl.BlockSpec(memory_space=pltpu.HBM)],
        [VMEM] * 5,
        [pltpu.SemaphoreType.DMA((32,))],
        moved=4 << 20,
    )
    other_block = after_all(other_block, packed)
    states = [sends[0]] + [shift_second(sends[d], d) for d in (1, 2, 3)]

    tokens = []
    arrived = (block, other_block)
    for step in range(5):
        if 0 < step < 4:
            awaited = {2: (states[1], states[3]), 3: (states[2],)}.get(step, ())
            awaited = (tokens[-1], *awaited)
            arrived = (arrived[0], after_all(arrived[1], *awaited))
        if step < 4:
            send = pass_on if step < 3 else pass_last
            after = (send(arrived[0]), send(arrived[1]))
        buffers, token = add_slot(step, *arrived, buffers)
        tokens.append(token)
        arrived = after

    keep, one, two, three = buffers
    peak, mass, past = past_part(queries, kv_cache, cache_lengths)
    one, two, three = shift_first(one, 1), shift_first(two, 2), shift_first(three, 3)
    square, narrow = shape((256, 256), f32), shape((256, 256), bf16)
    own, one, two, three = call(
        middle_kernel,
        (square, narrow, narrow, narrow),
        (place, keep, one, two, three, past, peak, mass),
        [SMEM] + [VMEM] * 4 + [ANY] * 3,
        [VMEM] * 4,
        moved=4 << 20,
    )
    one, two, three = shift_second(one, 1), shift_second(two, 2), shift_second(three, 3)
    gradient = own + one.astype(f32) + two.astype(f32) + three.astype(f32)
    gradient = gradient.astype(bf16)
    gradient = to_owner(gradient)
    new_master, new_first, new_second, weight = call(
        adam_kernel,
        (square, narrow, narrow, narrow),
        (gradient, master, first_moment, second_moment),
        [VMEM] * 4,
        [VMEM] * 4,
        moved=1 << 20,
    )

    pair = jnp.stack([weight, swap_core(weight)])
    line = [pair, shift_first(pair, -1), shift_first(pair, 2), shift_first(pair, 1)]
    result, sent = shape((count, 256), f32), shape((count, 256), bf16)
    own, one, two, three = call(
        project_kernel,
        (result, sent, sent, sent),
        (*line, *states),
        [VMEM] * 8,
        [VMEM] * 4,
        flops=2 * 16 * count * 512 * 256,
        moved=4 << 20,
    )
    one, two, three = shift_second(one, -1), shift_second(two, -2), shift_second(three, -3)
    attended = call(
        finish_kernel,
        shape((count, queries.shape[2]), bf16),
        (own, one, two, three, queries.reshape(count, queries.shape[2]), peak, mass, past),
        [VMEM] * 8,
        VMEM,
        moved=1 << 20,
    )
    return new_master, new_first, new_second, attended.reshape(queries.shape)


def solution(mesh):
    in_specs = (
        P(("fsdp", "rep"), "tp"),
        P(("fsdp", "rep"), "tp"),
        P(("fsdp", "rep"), "tp"),
        P(("fsdp", "rep"), "tp"),
        P(("fsdp", "rep"), "tp"),
        P(None, ("fsdp", "rep"), None),
        P(None, ("fsdp", "rep"), "tp"),
        P(("fsdp", "rep"), None, "tp"),
        P(("fsdp", "rep")),
    )
    out_specs = (
        P(("fsdp", "rep"), "tp"),
        P(("fsdp", "rep"), "tp"),
        P(("fsdp", "rep"), "tp"),
        P(None, ("fsdp", "rep"), "tp"),
    )
    return jax.shard_map(body, mesh=mesh, in_specs=in_specs, out_specs=out_specs, check_vma=False)
```
